256 devices in a mesh: mic: 8 (over x, y_lo), grid: 32 (over y_hi, z, core).
Axes of the slice: x: 4, y: 4 (y_hi: 2, y_lo: 2; y = y_hi * 2 + y_lo), z: 8, core: 2. Of those that a mesh axis runs over, the one named last changes fastest.
Arguments:
- samples: bfloat16 [32, 4096, 4096], P('grid', 'mic'), may hold values from -6 to 6
- mic_places: float32 [3, 4096], P(None, 'mic'), may hold values from -0.5 to 0.5
- grid_places: float32 [3, 16384], P(None, 'grid'), may hold values from -0.5 to 0.5
Outputs:
- beam_map: float32 [16384], P('grid')
The draws below stay inside these ranges and needn't reach their ends.
All inputs are finite; a program needn't handle non-finite values.
Results may differ from the reference program's by a relative error of at most 0.0077.
Values may be sent and summed in bfloat16 or wider, within the bound.
A program may use at most 64 MiB of HBM per device.

```python
import jax
import jax.numpy as jnp
from jax import lax

M = 4096
L = 4096
BIN = 512
GP_DEV = 512
SEGMENTS = 32
GRIDPTS = 16384
N_GRID = 32


def block_scale(rng, shape, cuts, least, largest):
    def one(position, shards_of):
        draws = jax.random.uniform(jax.random.fold_in(jax.random.fold_in(rng, 6), position), (shards_of,), jnp.float32, least / len(cuts), largest / len(cuts))
        return jnp.repeat(jnp.exp(draws), shape[position] // shards_of).reshape((-1,) + (1,) * (len(shape) - position - 1))

    level = one(*cuts[0])
    for cut in cuts[1:]:
        level = level * one(*cut)
    return level


def bell_draw(stream_key, shape, width, most, split=(), kind=jnp.bfloat16):
    array = width * jax.random.normal(stream_key, shape, jnp.float32)
    if split:
        array = array * block_scale(stream_key, shape, split, -0.22, 0.18)
    return jnp.clip(array, -most, most).astype(kind)


def setup_inputs(seed: int = 0) -> dict:
    streams_of = jax.random.split(jax.random.key(seed), 4)
    return {
        "samples": bell_draw(streams_of[0], (SEGMENTS, M, L), 1.0, 6.0, ((0, 32), (1, 8))),
        "mic_places": jnp.clip(jax.random.uniform(streams_of[1], (3, M), jnp.float32, -0.5, 0.5) * block_scale(streams_of[1], (3, M), ((1, 8),), -0.4, 0.0), -0.5, 0.5),
        "grid_places": jnp.clip(jax.random.uniform(streams_of[2], (3, GRIDPTS), jnp.float32, -0.5, 0.5) * block_scale(streams_of[2], (3, GRIDPTS), ((1, 32),), -0.4, 0.0), -0.5, 0.5),
    }


WAVENUMBER = 120.0

def dft_table():
    steps = jnp.arange(L, dtype=jnp.int32)
    window = 0.5 - 0.5 * jnp.cos(2.0 * jnp.pi * steps.astype(jnp.float32) / L)
    scale = jnp.sqrt(jnp.sum(window * window))
    theta = 2.0 * jnp.pi * (BIN * steps % L).astype(jnp.float32) / L
    table = jnp.stack([window * jnp.cos(theta) / scale, -window * jnp.sin(theta) / scale], axis=1)
    return table.astype(jnp.bfloat16)

def steering(grid_block, mic_block):
    delta_x = grid_block[0][:, None] - mic_block[0][None, :]
    delta_y = grid_block[1][:, None] - mic_block[1][None, :]
    delta_z = grid_block[2][:, None] + 1.5 - mic_block[2][None, :]
    phase = WAVENUMBER * jnp.sqrt(delta_x * delta_x + delta_y * delta_y + delta_z * delta_z)
    return (jnp.cos(phase).astype(jnp.bfloat16), jnp.sin(phase).astype(jnp.bfloat16))

def contract_last(left, right):
    return lax.dot_general(left, right, (((1,), (1,)), ((), ())), preferred_element_type=jnp.float32)

def reference(samples, mic_places, grid_places):
    table = dft_table()
    flat = jnp.dot(samples.reshape(-1, L), table, preferred_element_type=jnp.float32)
    spectra = flat.astype(jnp.bfloat16).reshape(SEGMENTS, M, 2)
    spec_real = spectra[:, :, 0]
    spec_imag = spectra[:, :, 1]
    real_f = spec_real.astype(jnp.float32)
    imag_f = spec_imag.astype(jnp.float32)
    power = jnp.sum(real_f * real_f + imag_f * imag_f)
    blocks = jnp.transpose(grid_places.reshape(3, N_GRID, GP_DEV), (1, 0, 2))

    def one_block(grid_block):
        cos_part, sin_part = steering(grid_block, mic_places)
        beam_real = contract_last(spec_real, cos_part) - contract_last(spec_imag, sin_part)
        beam_imag = contract_last(spec_imag, cos_part) + contract_last(spec_real, sin_part)
        return (lax.optimization_barrier(jnp.sum(beam_real * beam_real + beam_imag * beam_imag, axis=0)) - power) / (SEGMENTS * M)
    return lax.map(one_block, blocks).reshape(GRIDPTS)
```

```python
import jax
import jax.numpy as jnp
import ml_dtypes
import numpy as np
from jax import lax
from jax.experimental import pallas as pl
from jax.experimental.pallas import tpu as pltpu
from jax.sharding import PartitionSpec as P

L = 4096
BIN = 512
WAVENUMBER = 120.0
MESH = pl.DeviceIdType.MESH

NMIC = 8
NGRID = 32
NZ = 8
PARTS = 8
BATCHES = 4
SEGS = NGRID // BATCHES
TILES = 4


def dft_table():
    steps = np.arange(L, dtype=np.int64)
    window = (0.5 - 0.5 * np.cos(2.0 * np.pi * steps / L)).astype(np.float32)
    scale = np.sqrt(np.sum(window.astype(np.float64) ** 2)).astype(np.float32)
    theta = 2.0 * np.pi * ((BIN * steps) % L) / L
    real = window * np.cos(theta).astype(np.float32) / scale
    imag = -window * np.sin(theta).astype(np.float32) / scale
    rows = [real if (r % 8) < 4 else imag for r in range(16)]
    return np.stack(rows).astype(ml_dtypes.bfloat16)


def sine_cosine(turns):
    r = turns - jnp.round(turns)
    u = r * r
    s = SIN[-1]
    for coefficient in SIN[-2::-1]:
        s = s * u + coefficient
    s = s * r
    c = COS[-1]
    for coefficient in COS[-2::-1]:
        c = c * u + coefficient
    return s * c, 1.0 - s * s


def fitted():
    nodes = 0.125 - 0.125 * np.cos(np.pi * (np.arange(400) + 0.5) / 400)
    r = np.sqrt(nodes)
    sin_fit = np.polynomial.chebyshev.Chebyshev.fit(nodes, np.sqrt(2) * np.sin(np.pi * r) / r, 4, domain=[0, 0.25])
    cos_fit = np.polynomial.chebyshev.Chebyshev.fit(nodes, np.sqrt(2) * np.cos(np.pi * r), 4, domain=[0, 0.25])
    as_list = lambda fit: [float(v) for v in fit.convert(kind=np.polynomial.Polynomial).coef]
    return as_list(sin_fit), as_list(cos_fit)


SIN, COS = fitted()


def slot_of(grid):
    return (grid // 2 % NZ) * 4 + (grid // 16) * 2 + grid % 2


def grid_of(slot):
    return (slot // 2 % 2) * 16 + (slot // 4) * 2 + slot % 2


def kernel(
    samples, table_hbm, mic_hbm, grid_hbm, out_ref,
    parts, table, mic, grid, mic_columns, gather, unpacked, weights, beams,
    load_sem, small_sem, gsend, grecv, bsend, brecv,
):
    me_mic = lax.axis_index("mic")
    me_grid = lax.axis_index("grid")
    me = slot_of(me_grid)
    width = L // PARTS

    smalls = [
        pltpu.make_async_copy(src, dst, small_sem.at[i])
        for i, (src, dst) in enumerate([(table_hbm, table), (mic_hbm, mic), (grid_hbm, grid)])
    ]
    loads = [
        pltpu.make_async_copy(
            samples.at[0, :, pl.ds(p * width, width)], parts.at[p], load_sem.at[p]
        )
        for p in range(PARTS)
    ]
    smalls[0].start()
    for load in loads:
        load.start()
    smalls[1].start()
    smalls[2].start()

    barrier = pltpu.get_barrier_semaphore()

    def grid_peer(k):
        return lax.rem(me + k, NGRID)

    def mic_peer(k):
        return lax.rem(me_mic + k, NMIC)

    for k in range(1, NGRID):
        pl.semaphore_signal(
            barrier, inc=1, device_id=(me_mic, grid_of(grid_peer(k))), device_id_type=MESH
        )
    for k in range(1, NMIC):
        pl.semaphore_signal(
            barrier, inc=1, device_id=(mic_peer(k), me_grid), device_id_type=MESH
        )

    smalls[0].wait()
    total = jnp.zeros((16, 512), jnp.float32)
    for p in range(PARTS):
        loads[p].wait()
        total += lax.dot_general(
            table[:, p * width : (p + 1) * width],
            parts[p],
            (((1,), (1,)), ((), ())),
            preferred_element_type=jnp.float32,
        )
    total = total[:8]
    lane_block = lax.rem(lax.broadcasted_iota(jnp.int32, (8, 128), 0), 4)
    own = total[:, :128]
    for k in range(1, 4):
        own = jnp.where(lane_block == k, total[:, 128 * k : 128 * (k + 1)], own)
    gather[me] = own.astype(jnp.bfloat16)

    pl.semaphore_wait(barrier, NGRID + NMIC - 2)

    gather_copies = []
    for k in range(1, NGRID):
        copy = pltpu.make_async_remote_copy(
            src_ref=gather.at[me],
            dst_ref=gather.at[me],
            send_sem=gsend.at[k],
            recv_sem=grecv.at[me],
            device_id=(me_mic, grid_of(grid_peer(k))),
            device_id_type=MESH,
        )
        copy.start()
        gather_copies.append(copy)

    smalls[1].wait()
    smalls[2].wait()
    mic_columns[...] = jnp.concatenate(
        [mic[...], jnp.zeros((5, 512), jnp.float32)], axis=0
    ).T
    gx = grid[0:1, :]
    gy = grid[1:2, :]
    gz = grid[2:3, :] + 1.5
    rows = 32

    def steer(i, carry):
        at = pl.multiple_of(i * rows, rows)
        dx = gx - mic_columns[pl.ds(at, rows), 0:1]
        dy = gy - mic_columns[pl.ds(at, rows), 1:2]
        dz = gz - mic_columns[pl.ds(at, rows), 2:3]
        dist = jnp.sqrt(dx * dx + dy * dy + dz * dz)
        sine, cosine = sine_cosine(dist * (WAVENUMBER / (2.0 * np.pi)))
        weights[pl.ds(at, rows), :] = cosine.astype(jnp.bfloat16)
        weights[pl.ds(pl.multiple_of(at + 512, rows), rows), :] = sine.astype(jnp.bfloat16)
        return carry

    lax.fori_loop(0, 512 // rows, steer, 0)

    power = jnp.zeros((8, 128), jnp.float32)
    beam_copies = []
    for b in range(BATCHES):
        for s in range(b * SEGS, (b + 1) * SEGS):
            @pl.when(me != s)
            def _():
                pltpu.make_async_remote_copy(
                    src_ref=gather.at[s],
                    dst_ref=gather.at[s],
                    send_sem=gsend.at[0],
                    recv_sem=grecv.at[s],
                    device_id=(me_mic, me_grid),
                    device_id_type=MESH,
                ).wait_recv()
        block = gather[b * SEGS : (b + 1) * SEGS].astype(jnp.float32)
        power += jnp.sum(block * block, axis=0)
        unpacked[...] = block
        real = jnp.concatenate([unpacked[:, k, :] for k in range(4)], axis=1)
        imag = jnp.concatenate([unpacked[:, 4 + k, :] for k in range(4)], axis=1)
        left = jnp.concatenate(
            [
                jnp.concatenate([real, -imag], axis=1),
                jnp.concatenate([imag, real], axis=1),
            ],
            axis=0,
        ).astype(jnp.bfloat16)
        beam = jnp.dot(left, weights[...], preferred_element_type=jnp.float32)
        for q in range(4):
            beams[b, me_mic, q] = beam[:, 128 * q : 128 * (q + 1)].astype(jnp.bfloat16)
        tiles = TILES
        if b == BATCHES - 1:
            high = power.astype(jnp.bfloat16)
            low = (power - high.astype(jnp.float32)).astype(jnp.bfloat16)
            beams[b, me_mic, TILES] = jnp.concatenate([high, low], axis=0)
            tiles = TILES + 1
        for k in range(1, NMIC):
            copy = pltpu.make_async_remote_copy(
                src_ref=beams.at[b, me_mic, pl.ds(0, tiles)],
                dst_ref=beams.at[b, me_mic, pl.ds(0, tiles)],
                send_sem=bsend.at[b, k],
                recv_sem=brecv.at[b, me_mic],
                device_id=(mic_peer(k), me_grid),
                device_id_type=MESH,
            )
            copy.start()
            beam_copies.append(copy)

    sums = [jnp.zeros((8, 128), jnp.float32) for _ in range(4)]
    for b in range(BATCHES):
        tiles = TILES + 1 if b == BATCHES - 1 else TILES
        for j in range(NMIC):
            @pl.when(me_mic != j)
            def _():
                pltpu.make_async_remote_copy(
                    src_ref=beams.at[b, j, pl.ds(0, tiles)],
                    dst_ref=beams.at[b, j, pl.ds(0, tiles)],
                    send_sem=bsend.at[b, 0],
                    recv_sem=brecv.at[b, j],
                    device_id=(me_mic, me_grid),
                    device_id_type=MESH,
                ).wait_recv()
        for q in range(4):
            whole = beams[b, 0, q].astype(jnp.float32)
            for j in range(1, NMIC):
                whole += beams[b, j, q].astype(jnp.float32)
            whole = whole * whole
            sums[q] += whole[:8] + whole[8:]
    all_power = jnp.zeros((16, 128), jnp.float32)
    for j in range(NMIC):
        all_power += beams[BATCHES - 1, j, TILES].astype(jnp.float32)
    all_power = jnp.sum(all_power)
    for q in range(4):
        line = (jnp.sum(sums[q], axis=0) - all_power) * (1.0 / (NGRID * 512 * NMIC))
        out_ref[pl.ds(128 * q, 128)] = line

    for copy in gather_copies + beam_copies:
        copy.wait_send()


def per_device(samples, mic_places, grid_places):
    hbm = pl.BlockSpec(memory_space=pltpu.HBM)
    width = L // PARTS
    table = jnp.asarray(dft_table())
    return pl.pallas_call(
        kernel,
        out_shape=jax.ShapeDtypeStruct((512,), jnp.float32),
        in_specs=[hbm] * 4,
        out_specs=pl.BlockSpec(memory_space=pltpu.VMEM),
        scratch_shapes=[
            pltpu.VMEM((PARTS, 512, width), jnp.bfloat16),
            pltpu.VMEM((16, L), jnp.bfloat16),
            pltpu.VMEM((3, 512), jnp.float32),
            pltpu.VMEM((3, 512), jnp.float32),
            pltpu.VMEM((512, 8), jnp.float32),
            pltpu.VMEM((NGRID, 8, 128), jnp.bfloat16),
            pltpu.VMEM((SEGS, 8, 128), jnp.float32),
            pltpu.VMEM((1024, 512), jnp.bfloat16),
            pltpu.VMEM((BATCHES, NMIC, TILES + 1, 16, 128), jnp.bfloat16),
            pltpu.SemaphoreType.DMA((PARTS,)),
            pltpu.SemaphoreType.DMA((3,)),
            pltpu.SemaphoreType.DMA((NGRID,)),
            pltpu.SemaphoreType.DMA((NGRID,)),
            pltpu.SemaphoreType.DMA((BATCHES, NMIC)),
            pltpu.SemaphoreType.DMA((BATCHES, NMIC)),
        ],
        compiler_params=pltpu.CompilerParams(
            collective_id=0, has_side_effects=True, vmem_limit_bytes=32 * 1024 * 1024
        ),
    )(samples, table, mic_places, grid_places)


def solution(mesh):
    in_specs = (P("grid", "mic", None), P(None, "mic"), P(None, "grid"))
    return jax.shard_map(
        per_device, mesh=mesh, in_specs=in_specs, out_specs=P("grid"), check_vma=False
    )
```

```python
import jax
import jax.numpy as jnp
import ml_dtypes
import numpy as np
from jax import lax
from jax.experimental import pallas as pl
from jax.experimental.pallas import tpu as pltpu
from jax.sharding import PartitionSpec as P

L = 4096
BIN = 512
WAVENUMBER = 120.0
MESH = pl.DeviceIdType.MESH

NMIC = 8
NGRID = 32
NZ = 8
PARTS = 4
HALF = 4
CUBE = 16
BATCHES = ((0, 16), (0, 8), (8, 8))


def tiles_of(b):
    return BATCHES[b][1] // 2 + (b == len(BATCHES) - 1)


def dft_table():
    steps = np.arange(L, dtype=np.int64)
    window = (0.5 - 0.5 * np.cos(2.0 * np.pi * steps / L)).astype(np.float32)
    scale = np.sqrt(np.sum(window.astype(np.float64) ** 2)).astype(np.float32)
    theta = 2.0 * np.pi * ((BIN * steps) % L) / L
    cosine = np.round(np.cos(theta), 12)
    sine = np.round(np.sin(theta), 12)
    size = np.maximum(np.abs(cosine), np.abs(sine)).astype(np.float32)
    magnitude = (window * size / scale).astype(ml_dtypes.bfloat16).astype(np.float32)
    signs = [np.sign(cosine) if r < 4 else -np.sign(sine) for r in range(8)]
    return np.stack([magnitude] * 8), np.stack(signs)[:, :128].astype(np.float32)


def sine_cosine(turns):
    r = turns - jnp.round(turns)
    u = r * r
    s = SIN[-1]
    for coefficient in SIN[-2::-1]:
        s = s * u + coefficient
    s = s * r
    c = COS[-1]
    for coefficient in COS[-2::-1]:
        c = c * u + coefficient
    return s * c, 1.0 - s * s


def fitted():
    nodes = 0.125 - 0.125 * np.cos(np.pi * (np.arange(400) + 0.5) / 400)
    r = np.sqrt(nodes)
    sin_fit = np.polynomial.chebyshev.Chebyshev.fit(nodes, np.sqrt(2) * np.sin(np.pi * r) / r, 4, domain=[0, 0.25])
    cos_fit = np.polynomial.chebyshev.Chebyshev.fit(nodes, np.sqrt(2) * np.cos(np.pi * r), 4, domain=[0, 0.25])
    as_list = lambda fit: [float(v) for v in fit.convert(kind=np.polynomial.Polynomial).coef]
    return as_list(sin_fit), as_list(cos_fit)


SIN, COS = fitted()


def slot_of(grid):
    return (grid // 2 % NZ) * 4 + (grid // 16) * 2 + grid % 2


def grid_of(slot):
    return (slot // 2 % 2) * 16 + (slot // 4) * 2 + slot % 2


def kernel(
    samples, table_hbm, signs_hbm, mic_hbm, grid_hbm, out_ref,
    parts, table, signs, folded, mic, grid, mic_columns, gather, unpacked, weights, beams,
    load_sem, small_sem, gsend, grecv, bsend, brecv,
):
    me_mic = lax.axis_index("mic")
    me_grid = lax.axis_index("grid")
    me = slot_of(me_grid)
    height = 512 // PARTS

    smalls = [
        pltpu.make_async_copy(src, dst, small_sem.at[i])
        for i, (src, dst) in enumerate(
            [(table_hbm, table), (signs_hbm, signs), (mic_hbm, mic), (grid_hbm, grid)]
        )
    ]
    loads = [
        pltpu.make_async_copy(
            samples.at[0, pl.ds(p * height, height)],
            parts.at[pl.ds(p * height, height)],
            load_sem.at[p],
        )
        for p in range(PARTS)
    ]
    loads[0].start()
    smalls[0].start()
    for load in loads[1:]:
        load.start()
    for small in smalls[1:]:
        small.start()

    barrier = pltpu.get_barrier_semaphore()
    my_z = me // 4
    late = my_z // HALF
    own_base = late * CUBE

    def near(k):
        return own_base + lax.rem(me - own_base + k, CUBE)

    def across(k):
        z = jnp.where(late == 1, k // 4, NZ - 1 - k // 4)
        return z * 4 + lax.rem(me + k, 4)

    def mic_peer(k):
        return lax.rem(me_mic + k, NMIC)

    def signal(mic_index, slot):
        pl.semaphore_signal(
            barrier, inc=1, device_id=(mic_index, grid_of(slot)), device_id_type=MESH
        )

    @pl.when(late == 0)
    def _():
        for k in range(CUBE):
            signal(me_mic, across(k))

    for k in range(1, CUBE):
        signal(me_mic, near(k))
    for k in range(1, NMIC):
        signal(mic_peer(k), me)

    def spectra_copy(k, slot):
        return pltpu.make_async_remote_copy(
            src_ref=gather.at[me],
            dst_ref=gather.at[me],
            send_sem=gsend.at[k],
            recv_sem=grecv.at[me],
            device_id=(me_mic, grid_of(slot)),
            device_id_type=MESH,
        )

    def arrival(slot):
        return pltpu.make_async_remote_copy(
            src_ref=gather.at[slot],
            dst_ref=gather.at[slot],
            send_sem=gsend.at[0],
            recv_sem=grecv.at[slot],
            device_id=(me_mic, me_grid),
            device_id_type=MESH,
        )

    fold = 64

    def fold_rows(i, carry):
        at = pl.multiple_of(i * fold, fold)
        total = jnp.zeros((fold, 128), jnp.float32)
        for t in range(0, L, 128):
            factor = jnp.concatenate([table[:, t : t + 128]] * (fold // 8), axis=0)
            total += parts[pl.ds(at, fold), t : t + 128].astype(jnp.float32) * factor
        folded[pl.ds(at, fold), :] = total
        return carry

    smalls[0].wait()
    for p in range(PARTS):
        loads[p].wait()
        lax.fori_loop(p * height // fold, (p + 1) * height // fold, fold_rows, 0)
    smalls[1].wait()
    total = lax.dot_general(
        signs[...],
        folded[...],
        (((1,), (1,)), ((), ())),
        preferred_element_type=jnp.float32,
        precision=lax.Precision.HIGHEST,
    )
    lane_block = lax.rem(lax.broadcasted_iota(jnp.int32, (8, 128), 0), 4)
    own = total[:, :128]
    for k in range(1, 4):
        own = jnp.where(lane_block == k, total[:, 128 * k : 128 * (k + 1)], own)
    gather[me] = own.astype(jnp.bfloat16)

    pl.semaphore_wait(barrier, CUBE - 1 + NMIC - 1 + late * CUBE)

    @pl.when(late == 1)
    def _():
        for k in range(CUBE):
            spectra_copy(CUBE + k, across(k)).start()

    for k in range(1, CUBE):
        spectra_copy(k, near(k)).start()

    smalls[2].wait()
    smalls[3].wait()
    mic_columns[...] = jnp.concatenate(
        [mic[...], jnp.zeros((5, 512), jnp.float32)], axis=0
    ).T
    gx = grid[0:1, :]
    gy = grid[1:2, :]
    gz = grid[2:3, :] + 1.5
    step = 32

    def steer(i, carry):
        at = pl.multiple_of(i * step, step)
        dx = gx - mic_columns[pl.ds(at, step), 0:1]
        dy = gy - mic_columns[pl.ds(at, step), 1:2]
        dz = gz - mic_columns[pl.ds(at, step), 2:3]
        dist = jnp.sqrt(dx * dx + dy * dy + dz * dz)
        sine, cosine = sine_cosine(dist * (WAVENUMBER / (2.0 * np.pi)))
        weights[pl.ds(at, step), :] = cosine.astype(jnp.bfloat16)
        weights[pl.ds(pl.multiple_of(at + 512, step), step), :] = sine.astype(jnp.bfloat16)
        return carry

    lax.fori_loop(0, 512 // step, steer, 0)

    power = jnp.zeros((8, 128), jnp.float32)
    beam_copies = []
    for b, (start, segs) in enumerate(BATCHES):
        if b == 0:
            for k in range(1, CUBE):
                arrival(near(k)).wait_recv()
            first = own_base
        else:
            for k in range(start, start + segs):
                arrival(across(k)).wait_recv()
                if k == 0:
                    @pl.when(late == 0)
                    def _():
                        for i in range(CUBE):
                            spectra_copy(CUBE + i, across(i)).start()

            first = jnp.where(late == 1, start, NGRID - start - segs)
        rows = 2 * segs
        tiles = tiles_of(b)
        block = gather[pl.ds(first, segs)].astype(jnp.float32)
        power += jnp.sum(block * block, axis=0)
        unpacked[:segs] = block
        real = jnp.concatenate([unpacked[:segs, k, :] for k in range(4)], axis=1)
        imag = jnp.concatenate([unpacked[:segs, 4 + k, :] for k in range(4)], axis=1)
        left = jnp.concatenate(
            [
                jnp.concatenate([real, -imag], axis=1),
                jnp.concatenate([imag, real], axis=1),
            ],
            axis=0,
        ).astype(jnp.bfloat16)
        beam = jnp.dot(left, weights[...], preferred_element_type=jnp.float32)
        for i in range(rows // 16):
            for q in range(4):
                tile = beam[16 * i : 16 * (i + 1), 128 * q : 128 * (q + 1)]
                beams[b, me_mic, 4 * i + q] = tile.astype(jnp.bfloat16)
        if b == len(BATCHES) - 1:
            high = power.astype(jnp.bfloat16)
            low = (power - high.astype(jnp.float32)).astype(jnp.bfloat16)
            beams[b, me_mic, tiles - 1] = jnp.concatenate([high, low], axis=0)
        for k in range(1, NMIC):
            copy = pltpu.make_async_remote_copy(
                src_ref=beams.at[b, me_mic, pl.ds(0, tiles)],
                dst_ref=beams.at[b, me_mic, pl.ds(0, tiles)],
                send_sem=bsend.at[b, k],
                recv_sem=brecv.at[b, me_mic],
                device_id=(mic_peer(k), me_grid),
                device_id_type=MESH,
            )
            copy.start()
            beam_copies.append(copy)

    sums = [jnp.zeros((16, 128), jnp.float32) for _ in range(4)]
    for b, (start, segs) in enumerate(BATCHES):
        tiles = tiles_of(b)
        for j in range(NMIC):
            @pl.when(me_mic != j)
            def _():
                pltpu.make_async_remote_copy(
                    src_ref=beams.at[b, j, pl.ds(0, tiles)],
                    dst_ref=beams.at[b, j, pl.ds(0, tiles)],
                    send_sem=bsend.at[b, 0],
                    recv_sem=brecv.at[b, j],
                    device_id=(me_mic, me_grid),
                    device_id_type=MESH,
                ).wait_recv()
        for i in range(segs // 8):
            for q in range(4):
                whole = beams[b, 0, 4 * i + q].astype(jnp.float32)
                for j in range(1, NMIC):
                    whole += beams[b, j, 4 * i + q].astype(jnp.float32)
                sums[q] += whole * whole
    all_power = jnp.zeros((16, 128), jnp.float32)
    last = len(BATCHES) - 1
    for j in range(NMIC):
        all_power += beams[last, j, tiles_of(last) - 1].astype(jnp.float32)
    all_power = jnp.sum(all_power)
    for q in range(4):
        line = (jnp.sum(sums[q], axis=0) - all_power) * (1.0 / (NGRID * 512 * NMIC))
        out_ref[pl.ds(128 * q, 128)] = line

    for k in range(1, 2 * CUBE):
        spectra_copy(k, me).wait_send()
    for copy in beam_copies:
        copy.wait_send()


def per_device(samples, mic_places, grid_places):
    hbm = pl.BlockSpec(memory_space=pltpu.HBM)
    table, signs = dft_table()
    return pl.pallas_call(
        kernel,
        out_shape=pltpu.VMEM((512,), jnp.float32),
        in_specs=[hbm] * 5,
        out_specs=pl.BlockSpec(memory_space=pltpu.VMEM),
        scratch_shapes=[
            pltpu.VMEM((512, L), jnp.bfloat16),
            pltpu.VMEM((8, L), jnp.float32),
            pltpu.VMEM((8, 128), jnp.float32),
            pltpu.VMEM((512, 128), jnp.float32),
            pltpu.VMEM((3, 512), jnp.float32),
            pltpu.VMEM((3, 512), jnp.float32),
            pltpu.VMEM((512, 8), jnp.float32),
            pltpu.VMEM((NGRID, 8, 128), jnp.bfloat16),
            pltpu.VMEM((CUBE, 8, 128), jnp.float32),
            pltpu.VMEM((1024, 512), jnp.bfloat16),
            pltpu.VMEM((len(BATCHES), NMIC, 8, 16, 128), jnp.bfloat16),
            pltpu.SemaphoreType.DMA((PARTS,)),
            pltpu.SemaphoreType.DMA((4,)),
            pltpu.SemaphoreType.DMA((NGRID,)),
            pltpu.SemaphoreType.DMA((NGRID,)),
            pltpu.SemaphoreType.DMA((len(BATCHES), NMIC)),
            pltpu.SemaphoreType.DMA((len(BATCHES), NMIC)),
        ],
        compiler_params=pltpu.CompilerParams(
            collective_id=0, has_side_effects=True, vmem_limit_bytes=60 * 1024 * 1024
        ),
    )(samples, jnp.asarray(table), jnp.asarray(signs), mic_places, grid_places)


def solution(mesh):
    in_specs = (P("grid", "mic", None), P(None, "mic"), P(None, "grid"))
    return jax.shard_map(
        per_device, mesh=mesh, in_specs=in_specs, out_specs=P("grid"), check_vma=False
    )
```

```python
import jax
import jax.numpy as jnp
import ml_dtypes
import numpy as np
from jax import lax
from jax.experimental import pallas as pl
from jax.experimental.pallas import tpu as pltpu
from jax.sharding import PartitionSpec as P

L = 4096
BIN = 512
WAVENUMBER = 120.0
MESH = pl.DeviceIdType.MESH

NMIC = 8
NGRID = 32
NZ = 8
PARTS = 4
HALF = 4
CUBE = 16
BATCHES = ((0, 0, 8), (0, 8, 8), (1, 0, 8), (1, 8, 8))


def tiles_of(b):
    return BATCHES[b][2] // 2 + (b == len(BATCHES) - 1)


def dft_table():
    steps = np.arange(L, dtype=np.int64)
    window = (0.5 - 0.5 * np.cos(2.0 * np.pi * steps / L)).astype(np.float32)
    scale = np.sqrt(np.sum(window.astype(np.float64) ** 2)).astype(np.float32)
    theta = 2.0 * np.pi * ((BIN * steps) % L) / L
    cosine = np.round(np.cos(theta), 12)
    sine = np.round(np.sin(theta), 12)
    size = np.maximum(np.abs(cosine), np.abs(sine)).astype(np.float32)
    magnitude = (window * size / scale).astype(ml_dtypes.bfloat16).astype(np.float32)
    signs = [np.sign(cosine) if r < 4 else -np.sign(sine) for r in range(8)]
    return np.stack([magnitude] * 8), np.stack(signs)[:, :128].astype(np.float32)


def sine_cosine(turns):
    r = turns - jnp.round(turns)
    u = r * r
    s = SIN[-1]
    for coefficient in SIN[-2::-1]:
        s = s * u + coefficient
    s = s * r
    c = COS[-1]
    for coefficient in COS[-2::-1]:
        c = c * u + coefficient
    return s * c, 1.0 - s * s


def fitted():
    nodes = 0.125 - 0.125 * np.cos(np.pi * (np.arange(400) + 0.5) / 400)
    r = np.sqrt(nodes)
    sin_fit = np.polynomial.chebyshev.Chebyshev.fit(nodes, np.sqrt(2) * np.sin(np.pi * r) / r, 4, domain=[0, 0.25])
    cos_fit = np.polynomial.chebyshev.Chebyshev.fit(nodes, np.sqrt(2) * np.cos(np.pi * r), 4, domain=[0, 0.25])
    as_list = lambda fit: [float(v) for v in fit.convert(kind=np.polynomial.Polynomial).coef]
    return as_list(sin_fit), as_list(cos_fit)


SIN, COS = fitted()


def slot_of(grid):
    return (grid // 2 % NZ) * 4 + (grid // 16) * 2 + grid % 2


def grid_of(slot):
    return (slot // 2 % 2) * 16 + (slot // 4) * 2 + slot % 2


def kernel(
    samples, table_hbm, signs_hbm, mic_hbm, grid_hbm, out_ref,
    parts, table, signs, folded, mic, grid, mic_columns, gather, unpacked, weights, beams,
    load_sem, small_sem, gsend, grecv, bsend, brecv,
):
    me_mic = lax.axis_index("mic")
    me_grid = lax.axis_index("grid")
    me = slot_of(me_grid)
    height = 512 // PARTS

    smalls = [
        pltpu.make_async_copy(src, dst, small_sem.at[i])
        for i, (src, dst) in enumerate(
            [(table_hbm, table), (signs_hbm, signs), (mic_hbm, mic), (grid_hbm, grid)]
        )
    ]
    loads = [
        pltpu.make_async_copy(
            samples.at[0, pl.ds(p * height, height)],
            parts.at[pl.ds(p * height, height)],
            load_sem.at[p],
        )
        for p in range(PARTS)
    ]
    loads[0].start()
    smalls[0].start()
    for load in loads[1:]:
        load.start()
    for small in smalls[1:]:
        small.start()

    barrier = pltpu.get_barrier_semaphore()
    my_z = me // 4
    late = my_z // HALF
    own_base = late * CUBE

    def near(k):
        return own_base + lax.rem(me - own_base + k, CUBE)

    upwards = jnp.where(late == 1, 1, (me // 4) // 2)

    def across(k):
        z = jnp.where(upwards == 1, k // 4, HALF - 1 - k // 4)
        return CUBE - own_base + z * 4 + lax.rem(me + k, 4)

    mic_steps = [(2, 1), (2, 0), (1, 1), (3, 1), (1, 0), (3, 0), (0, 1)]

    def mic_peer(k):
        step, other = mic_steps[k - 1]
        return lax.rem(me_mic // 2 + step, 4) * 2 + lax.rem(me_mic + other, 2)

    def signal(mic_index, slot):
        pl.semaphore_signal(
            barrier, inc=1, device_id=(mic_index, grid_of(slot)), device_id_type=MESH
        )

    @pl.when(late == 0)
    def _():
        for k in range(CUBE):
            signal(me_mic, across(k))

    for k in range(1, CUBE):
        signal(me_mic, near(k))
    for k in range(1, NMIC):
        signal(mic_peer(k), me)

    def spectra_copy(k, slot):
        return pltpu.make_async_remote_copy(
            src_ref=gather.at[me],
            dst_ref=gather.at[me],
            send_sem=gsend.at[k],
            recv_sem=grecv.at[me],
            device_id=(me_mic, grid_of(slot)),
            device_id_type=MESH,
        )

    def arrival(slot):
        return pltpu.make_async_remote_copy(
            src_ref=gather.at[slot],
            dst_ref=gather.at[slot],
            send_sem=gsend.at[0],
            recv_sem=grecv.at[slot],
            device_id=(me_mic, me_grid),
            device_id_type=MESH,
        )

    fold = 64

    def fold_rows(i, carry):
        at = pl.multiple_of(i * fold, fold)
        total = jnp.zeros((fold, 128), jnp.float32)
        for t in range(0, L, 128):
            factor = jnp.concatenate([table[:, t : t + 128]] * (fold // 8), axis=0)
            total += parts[pl.ds(at, fold), t : t + 128].astype(jnp.float32) * factor
        folded[pl.ds(at, fold), :] = total
        return carry

    smalls[0].wait()
    for p in range(PARTS):
        loads[p].wait()
        lax.fori_loop(p * height // fold, (p + 1) * height // fold, fold_rows, 0)
    smalls[1].wait()
    total = lax.dot_general(
        signs[...],
        folded[...],
        (((1,), (1,)), ((), ())),
        preferred_element_type=jnp.float32,
        precision=lax.Precision.HIGHEST,
    )
    lane_block = lax.rem(lax.broadcasted_iota(jnp.int32, (8, 128), 0), 4)
    own = total[:, :128]
    for k in range(1, 4):
        own = jnp.where(lane_block == k, total[:, 128 * k : 128 * (k + 1)], own)
    gather[me] = own.astype(jnp.bfloat16)

    pl.semaphore_wait(barrier, CUBE - 1 + NMIC - 1 + late * CUBE)

    @pl.when(late == 1)
    def _():
        for k in range(CUBE):
            spectra_copy(CUBE + k, across(k)).start()

    for k in range(1, CUBE):
        spectra_copy(k, near(k)).start()

    smalls[2].wait()
    smalls[3].wait()
    mic_columns[...] = jnp.concatenate(
        [mic[...], jnp.zeros((5, 512), jnp.float32)], axis=0
    ).T
    gx = grid[0:1, :]
    gy = grid[1:2, :]
    gz = grid[2:3, :] + 1.5
    step = 32

    def steer(i, carry):
        at = pl.multiple_of(i * step, step)
        dx = gx - mic_columns[pl.ds(at, step), 0:1]
        dy = gy - mic_columns[pl.ds(at, step), 1:2]
        dz = gz - mic_columns[pl.ds(at, step), 2:3]
        dist = jnp.sqrt(dx * dx + dy * dy + dz * dz)
        sine, cosine = sine_cosine(dist * (WAVENUMBER / (2.0 * np.pi)))
        weights[pl.ds(at, step), :] = cosine.astype(jnp.bfloat16)
        weights[pl.ds(pl.multiple_of(at + 512, step), step), :] = sine.astype(jnp.bfloat16)
        return carry

    lax.fori_loop(0, 512 // step, steer, 0)

    def tile_of(beam, t):
        if beam.shape[0] == 8:
            return jnp.concatenate(
                [beam[:, 256 * t : 256 * t + 128], beam[:, 256 * t + 128 : 256 * (t + 1)]], axis=0
            )
        i, q = t // 4, t % 4
        return beam[16 * i : 16 * (i + 1), 128 * q : 128 * (q + 1)]

    power = jnp.zeros((8, 128), jnp.float32)
    beam_copies = []
    for b, (far, start, segs) in enumerate(BATCHES):
        if not far:
            first = own_base + start
            for k in range(segs):
                @pl.when(me != first + k)
                def _():
                    arrival(first + k).wait_recv()
        else:
            for k in range(start, start + segs):
                arrival(across(k)).wait_recv()
                if k == 0:
                    @pl.when(late == 0)
                    def _():
                        for i in range(CUBE):
                            spectra_copy(CUBE + i, across(i)).start()

            first = CUBE - own_base + jnp.where(upwards == 1, start, CUBE - start - segs)
        tiles = tiles_of(b)
        block = gather[pl.ds(first, segs)].astype(jnp.float32)
        power += jnp.sum(block * block, axis=0)
        unpacked[:segs] = block
        real = jnp.concatenate([unpacked[:segs, k, :] for k in range(4)], axis=1)
        imag = jnp.concatenate([unpacked[:segs, 4 + k, :] for k in range(4)], axis=1)
        left = jnp.concatenate(
            [
                jnp.concatenate([real, -imag], axis=1),
                jnp.concatenate([imag, real], axis=1),
            ],
            axis=0,
        ).astype(jnp.bfloat16)
        beam = jnp.dot(left, weights[...], preferred_element_type=jnp.float32)
        for t in range(segs // 2):
            beams[b, me_mic, t] = tile_of(beam, t).astype(jnp.bfloat16)
        if b == len(BATCHES) - 1:
            high = power.astype(jnp.bfloat16)
            low = (power - high.astype(jnp.float32)).astype(jnp.bfloat16)
            beams[b, me_mic, tiles - 1] = jnp.concatenate([high, low], axis=0)
        for k in range(1, NMIC):
            copy = pltpu.make_async_remote_copy(
                src_ref=beams.at[b, me_mic, pl.ds(0, tiles)],
                dst_ref=beams.at[b, me_mic, pl.ds(0, tiles)],
                send_sem=bsend.at[b, k],
                recv_sem=brecv.at[b, me_mic],
                device_id=(mic_peer(k), me_grid),
                device_id_type=MESH,
            )
            copy.start()
            beam_copies.append(copy)

    for k in range(1, 2 * CUBE):
        spectra_copy(k, me).wait_send()
    for copy in beam_copies[: -(NMIC - 1)]:
        copy.wait_send()

    sums = [jnp.zeros((8, 128), jnp.float32) for _ in range(4)]
    for b, (far, start, segs) in enumerate(BATCHES):
        tiles = tiles_of(b)
        for j in range(NMIC):
            @pl.when(me_mic != j)
            def _():
                pltpu.make_async_remote_copy(
                    src_ref=beams.at[b, j, pl.ds(0, tiles)],
                    dst_ref=beams.at[b, j, pl.ds(0, tiles)],
                    send_sem=bsend.at[b, 0],
                    recv_sem=brecv.at[b, j],
                    device_id=(me_mic, me_grid),
                    device_id_type=MESH,
                ).wait_recv()
        for t in range(segs // 2):
            whole = beams[b, 0, t].astype(jnp.float32)
            for j in range(1, NMIC):
                whole += beams[b, j, t].astype(jnp.float32)
            whole = whole * whole
            if segs == 4:
                sums[2 * t] += whole[:8]
                sums[2 * t + 1] += whole[8:]
            else:
                sums[t % 4] += whole[:8] + whole[8:]
    all_power = jnp.zeros((16, 128), jnp.float32)
    last = len(BATCHES) - 1
    for j in range(NMIC):
        all_power += beams[last, j, tiles_of(last) - 1].astype(jnp.float32)
    all_power = jnp.sum(all_power)
    for q in range(4):
        line = (jnp.sum(sums[q], axis=0) - all_power) * (1.0 / (NGRID * 512 * NMIC))
        out_ref[pl.ds(128 * q, 128)] = line

    for copy in beam_copies[-(NMIC - 1) :]:
        copy.wait_send()


def per_device(samples, mic_places, grid_places):
    hbm = pl.BlockSpec(memory_space=pltpu.HBM)
    table, signs = dft_table()
    return pl.pallas_call(
        kernel,
        out_shape=pltpu.VMEM((512,), jnp.float32),
        in_specs=[hbm] * 5,
        out_specs=pl.BlockSpec(memory_space=pltpu.VMEM),
        scratch_shapes=[
            pltpu.VMEM((512, L), jnp.bfloat16),
            pltpu.VMEM((8, L), jnp.float32),
            pltpu.VMEM((8, 128), jnp.float32),
            pltpu.VMEM((512, 128), jnp.float32),
            pltpu.VMEM((3, 512), jnp.float32),
            pltpu.VMEM((3, 512), jnp.float32),
            pltpu.VMEM((512, 8), jnp.float32),
            pltpu.VMEM((NGRID, 8, 128), jnp.bfloat16),
            pltpu.VMEM((CUBE, 8, 128), jnp.float32),
            pltpu.VMEM((1024, 512), jnp.bfloat16),
            pltpu.VMEM((len(BATCHES), NMIC, 8, 16, 128), jnp.bfloat16),
            pltpu.SemaphoreType.DMA((PARTS,)),
            pltpu.SemaphoreType.DMA((4,)),
            pltpu.SemaphoreType.DMA((NGRID,)),
            pltpu.SemaphoreType.DMA((NGRID,)),
            pltpu.SemaphoreType.DMA((len(BATCHES), NMIC)),
            pltpu.SemaphoreType.DMA((len(BATCHES), NMIC)),
        ],
        compiler_params=pltpu.CompilerParams(
            collective_id=0, has_side_effects=True, vmem_limit_bytes=60 * 1024 * 1024
        ),
    )(samples, jnp.asarray(table), jnp.asarray(signs), mic_places, grid_places)


def solution(mesh):
    in_specs = (P("grid", "mic", None), P(None, "mic"), P(None, "grid"))
    return jax.shard_map(
        per_device, mesh=mesh, in_specs=in_specs, out_specs=P("grid"), check_vma=False
    )
```

```python
import jax
import jax.numpy as jnp
import ml_dtypes
import numpy as np
from jax import lax
from jax.experimental import pallas as pl
from jax.experimental.pallas import tpu as pltpu
from jax.sharding import PartitionSpec as P

L = 4096
BIN = 512
WAVENUMBER = 120.0
MESH = pl.DeviceIdType.MESH

NMIC = 8
NGRID = 32
NZ = 8
PARTS = 4
HALF = 4
CUBE = 16
BATCHES = ((0, 0, 8), (0, 8, 8), (1, 0, 8), (1, 8, 8))


def tiles_of(b):
    return BATCHES[b][2] // 2 + (b == len(BATCHES) - 1)


def dft_table():
    steps = np.arange(L, dtype=np.int64)
    window = (0.5 - 0.5 * np.cos(2.0 * np.pi * steps / L)).astype(np.float32)
    scale = np.sqrt(np.sum(window.astype(np.float64) ** 2)).astype(np.float32)
    theta = 2.0 * np.pi * ((BIN * steps) % L) / L
    cosine = np.round(np.cos(theta), 12)
    sine = np.round(np.sin(theta), 12)
    size = np.maximum(np.abs(cosine), np.abs(sine)).astype(np.float32)
    magnitude = (window * size / scale).astype(ml_dtypes.bfloat16).astype(np.float32)
    signs = [np.sign(cosine) if r < 4 else -np.sign(sine) for r in range(8)]
    return np.stack([magnitude] * 8), np.stack(signs)[:, :128].astype(np.float32)


def sine_cosine(turns):
    r = turns - jnp.round(turns)
    u = r * r
    s = SIN[-1]
    for coefficient in SIN[-2::-1]:
        s = s * u + coefficient
    s = s * r
    c = COS[-1]
    for coefficient in COS[-2::-1]:
        c = c * u + coefficient
    return s * c, 1.0 - s * s


def fitted():
    nodes = 0.125 - 0.125 * np.cos(np.pi * (np.arange(400) + 0.5) / 400)
    r = np.sqrt(nodes)
    sin_fit = np.polynomial.chebyshev.Chebyshev.fit(nodes, np.sqrt(2) * np.sin(np.pi * r) / r, 4, domain=[0, 0.25])
    cos_fit = np.polynomial.chebyshev.Chebyshev.fit(nodes, np.sqrt(2) * np.cos(np.pi * r), 4, domain=[0, 0.25])
    as_list = lambda fit: [float(v) for v in fit.convert(kind=np.polynomial.Polynomial).coef]
    return as_list(sin_fit), as_list(cos_fit)


SIN, COS = fitted()


def slot_of(grid):
    return (grid // 2 % NZ) * 4 + (grid // 16) * 2 + grid % 2


def grid_of(slot):
    return (slot // 2 % 2) * 16 + (slot // 4) * 2 + slot % 2


def kernel(
    samples, table_hbm, signs_hbm, mic_hbm, grid_hbm, out_ref,
    parts, table, signs, folded, mic, grid, mic_columns, gather, unpacked, weights, beams,
    load_sem, small_sem, gsend, grecv, bsend, brecv,
):
    me_mic = lax.axis_index("mic")
    me_grid = lax.axis_index("grid")
    me = slot_of(me_grid)
    height = 512 // PARTS

    smalls = [
        pltpu.make_async_copy(src, dst, small_sem.at[i])
        for i, (src, dst) in enumerate(
            [(table_hbm, table), (signs_hbm, signs), (mic_hbm, mic), (grid_hbm, grid)]
        )
    ]
    loads = [
        pltpu.make_async_copy(
            samples.at[0, pl.ds(p * height, height)],
            parts.at[pl.ds(p * height, height)],
            load_sem.at[p],
        )
        for p in range(PARTS)
    ]
    loads[0].start()
    smalls[0].start()
    for load in loads[1:]:
        load.start()
    for small in smalls[1:]:
        small.start()

    barrier = pltpu.get_barrier_semaphore()
    my_z = me // 4
    late = my_z // HALF
    own_base = late * CUBE

    def near(k):
        return own_base + lax.rem(me - own_base + k, CUBE)

    upwards = jnp.where(late == 1, 1, (me // 4) // 2)

    spot = lax.rem(me, 4)

    def across(k):
        z = jnp.where(upwards == 1, k // 4, HALF - 1 - k // 4)
        return CUBE - own_base + z * 4 + place(k % 4)

    def place(k):
        return (3 - spot, lax.rem(spot + 2, 4), spot + 1 - 2 * lax.rem(spot, 2), spot)[k]

    mic_steps = [(2, 1), (2, 0), (1, 1), (3, 1), (1, 0), (3, 0), (0, 1)]

    def mic_peer(k):
        step, other = mic_steps[k - 1]
        return lax.rem(me_mic // 2 + step, 4) * 2 + lax.rem(me_mic + other, 2)

    def signal(mic_index, slot):
        pl.semaphore_signal(
            barrier, inc=1, device_id=(mic_index, grid_of(slot)), device_id_type=MESH
        )

    @pl.when(late == 0)
    def _():
        for k in range(CUBE):
            signal(me_mic, across(k))

    for k in range(1, CUBE):
        signal(me_mic, near(k))
    for k in range(1, NMIC):
        signal(mic_peer(k), me)

    def spectra_copy(slot, semaphore):
        return pltpu.make_async_remote_copy(
            src_ref=gather.at[me],
            dst_ref=gather.at[me],
            send_sem=gsend,
            recv_sem=grecv.at[semaphore],
            device_id=(me_mic, grid_of(slot)),
            device_id_type=MESH,
        )

    def spectra_wait(first, count, semaphore):
        return pltpu.make_async_remote_copy(
            src_ref=gather.at[pl.ds(first, count)],
            dst_ref=gather.at[pl.ds(first, count)],
            send_sem=gsend,
            recv_sem=grecv.at[semaphore],
            device_id=(me_mic, me_grid),
            device_id_type=MESH,
        )

    my_batch = me // 8

    def crossing(k):
        nearest = jnp.where(k // 4 < HALF // 2, NZ - 1, HALF)
        first = (late == 1) & (me // 4 == nearest) & (k % 4 == 3)
        return jnp.where(first, 4, my_batch)

    fold = 64

    def fold_rows(i, carry):
        at = pl.multiple_of(i * fold, fold)
        total = jnp.zeros((fold, 128), jnp.float32)
        for t in range(0, L, 128):
            factor = jnp.concatenate([table[:, t : t + 128]] * (fold // 8), axis=0)
            total += parts[pl.ds(at, fold), t : t + 128].astype(jnp.float32) * factor
        folded[pl.ds(at, fold), :] = total
        return carry

    smalls[0].wait()
    for p in range(PARTS):
        loads[p].wait()
        lax.fori_loop(p * height // fold, (p + 1) * height // fold, fold_rows, 0)
    smalls[1].wait()
    total = lax.dot_general(
        signs[...],
        folded[...],
        (((1,), (1,)), ((), ())),
        preferred_element_type=jnp.float32,
        precision=lax.Precision.HIGHEST,
    )
    lane_block = lax.rem(lax.broadcasted_iota(jnp.int32, (8, 128), 0), 4)
    own = total[:, :128]
    for k in range(1, 4):
        own = jnp.where(lane_block == k, total[:, 128 * k : 128 * (k + 1)], own)
    gather[me] = own.astype(jnp.bfloat16)

    pl.semaphore_wait(barrier, CUBE - 1 + NMIC - 1 + late * CUBE)

    @pl.when(late == 1)
    def _():
        for k in range(CUBE):
            spectra_copy(across(k), crossing(k)).start()

    for k in range(1, CUBE):
        spectra_copy(near(k), my_batch).start()

    smalls[2].wait()
    smalls[3].wait()
    mic_columns[...] = jnp.concatenate(
        [mic[...], jnp.zeros((5, 512), jnp.float32)], axis=0
    ).T
    gx = grid[0:1, :]
    gy = grid[1:2, :]
    gz = grid[2:3, :] + 1.5
    step = 32

    def steer(i, carry):
        at = pl.multiple_of(i * step, step)
        dx = gx - mic_columns[pl.ds(at, step), 0:1]
        dy = gy - mic_columns[pl.ds(at, step), 1:2]
        dz = gz - mic_columns[pl.ds(at, step), 2:3]
        dist = jnp.sqrt(dx * dx + dy * dy + dz * dz)
        sine, cosine = sine_cosine(dist * (WAVENUMBER / (2.0 * np.pi)))
        weights[pl.ds(at, step), :] = cosine.astype(jnp.bfloat16)
        weights[pl.ds(pl.multiple_of(at + 512, step), step), :] = sine.astype(jnp.bfloat16)
        return carry

    lax.fori_loop(0, 512 // step, steer, 0)

    def tile_of(beam, t):
        if beam.shape[0] == 8:
            return jnp.concatenate(
                [beam[:, 256 * t : 256 * t + 128], beam[:, 256 * t + 128 : 256 * (t + 1)]], axis=0
            )
        i, q = t // 4, t % 4
        return beam[16 * i : 16 * (i + 1), 128 * q : 128 * (q + 1)]

    def beam_copy(b, slot, peer):
        tiles = tiles_of(b)
        return pltpu.make_async_remote_copy(
            src_ref=beams.at[b, slot, pl.ds(0, tiles)],
            dst_ref=beams.at[b, slot, pl.ds(0, tiles)],
            send_sem=bsend.at[b],
            recv_sem=brecv.at[b],
            device_id=(peer, me_grid),
            device_id_type=MESH,
        )

    def beam_wait(b):
        return beam_copy(b, pl.ds(0, NMIC - 1), me_mic)

    last = len(BATCHES) - 1
    power = jnp.zeros((8, 128), jnp.float32)
    for b, (far, start, segs) in enumerate(BATCHES):
        if far:
            first = CUBE - own_base + jnp.where(upwards == 1, start, CUBE - start - segs)
        else:
            first = own_base + start
        short = my_batch == first // 8
        if far and start == 0:
            @pl.when(late == 0)
            def _():
                spectra_wait(first, 1, 4).wait_recv()
                for k in range(CUBE):
                    spectra_copy(across(k), my_batch).start()

            short = late == 0

        @pl.when(short)
        def _():
            spectra_wait(first, segs - 1, first // 8).wait_recv()

        @pl.when(jnp.logical_not(short))
        def _():
            spectra_wait(first, segs, first // 8).wait_recv()

        tiles = tiles_of(b)
        block = gather[pl.ds(first, segs)].astype(jnp.float32)
        power += jnp.sum(block * block, axis=0)
        unpacked[:segs] = block
        real = jnp.concatenate([unpacked[:segs, k, :] for k in range(4)], axis=1)
        imag = jnp.concatenate([unpacked[:segs, 4 + k, :] for k in range(4)], axis=1)
        left = jnp.concatenate(
            [
                jnp.concatenate([real, -imag], axis=1),
                jnp.concatenate([imag, real], axis=1),
            ],
            axis=0,
        ).astype(jnp.bfloat16)
        beam = jnp.dot(left, weights[...], preferred_element_type=jnp.float32)
        for t in range(segs // 2):
            beams[b, me_mic, t] = tile_of(beam, t).astype(jnp.bfloat16)
        if b == len(BATCHES) - 1:
            high = power.astype(jnp.bfloat16)
            low = (power - high.astype(jnp.float32)).astype(jnp.bfloat16)
            beams[b, me_mic, tiles - 1] = jnp.concatenate([high, low], axis=0)
        for k in range(1, NMIC):
            beam_copy(b, me_mic, mic_peer(k)).start()

    spectra_wait(0, 2 * CUBE - 1, 0).wait_send()
    for b in range(last):
        beam_wait(b).wait_send()

    sums = [jnp.zeros((8, 128), jnp.float32) for _ in range(4)]
    for b, (far, start, segs) in enumerate(BATCHES):
        tiles = tiles_of(b)
        beam_wait(b).wait_recv()
        for t in range(segs // 2):
            whole = beams[b, 0, t].astype(jnp.float32)
            for j in range(1, NMIC):
                whole += beams[b, j, t].astype(jnp.float32)
            whole = whole * whole
            if segs == 4:
                sums[2 * t] += whole[:8]
                sums[2 * t + 1] += whole[8:]
            else:
                sums[t % 4] += whole[:8] + whole[8:]
    all_power = jnp.zeros((16, 128), jnp.float32)
    for j in range(NMIC):
        all_power += beams[last, j, tiles_of(last) - 1].astype(jnp.float32)
    all_power = jnp.sum(all_power)
    for q in range(4):
        line = (jnp.sum(sums[q], axis=0) - all_power) * (1.0 / (NGRID * 512 * NMIC))
        out_ref[pl.ds(128 * q, 128)] = line

    beam_wait(last).wait_send()


def per_device(samples, mic_places, grid_places):
    hbm = pl.BlockSpec(memory_space=pltpu.HBM)
    table, signs = dft_table()
    return pl.pallas_call(
        kernel,
        out_shape=pltpu.VMEM((512,), jnp.float32),
        in_specs=[hbm] * 5,
        out_specs=pl.BlockSpec(memory_space=pltpu.VMEM),
        scratch_shapes=[
            pltpu.VMEM((512, L), jnp.bfloat16),
            pltpu.VMEM((8, L), jnp.float32),
            pltpu.VMEM((8, 128), jnp.float32),
            pltpu.VMEM((512, 128), jnp.float32),
            pltpu.VMEM((3, 512), jnp.float32),
            pltpu.VMEM((3, 512), jnp.float32),
            pltpu.VMEM((512, 8), jnp.float32),
            pltpu.VMEM((NGRID, 8, 128), jnp.bfloat16),
            pltpu.VMEM((CUBE, 8, 128), jnp.float32),
            pltpu.VMEM((1024, 512), jnp.bfloat16),
            pltpu.VMEM((len(BATCHES), NMIC, 8, 16, 128), jnp.bfloat16),
            pltpu.SemaphoreType.DMA((PARTS,)),
            pltpu.SemaphoreType.DMA((4,)),
            pltpu.SemaphoreType.DMA,
            pltpu.SemaphoreType.DMA((5,)),
            pltpu.SemaphoreType.DMA((len(BATCHES),)),
            pltpu.SemaphoreType.DMA((len(BATCHES),)),
        ],
        compiler_params=pltpu.CompilerParams(
            collective_id=0, has_side_effects=True, vmem_limit_bytes=60 * 1024 * 1024
        ),
    )(samples, jnp.asarray(table), jnp.asarray(signs), mic_places, grid_places)


def solution(mesh):
    in_specs = (P("grid", "mic", None), P(None, "mic"), P(None, "grid"))
    return jax.shard_map(
        per_device, mesh=mesh, in_specs=in_specs, out_specs=P("grid"), check_vma=False
    )
```

```python
import jax
import jax.numpy as jnp
import ml_dtypes
import numpy as np
from jax import lax
from jax.experimental import pallas as pl
from jax.experimental.pallas import tpu as pltpu
from jax.sharding import PartitionSpec as P

L = 4096
BIN = 512
WAVENUMBER = 120.0
MESH = pl.DeviceIdType.MESH

NMIC = 8
NGRID = 32
NZ = 8
PARTS = 4
HALF = 4
CUBE = 16
BATCHES = ((0, 0, 8), (0, 8, 8), (1, 0, 8), (1, 8, 8))


def tiles_of(b):
    return BATCHES[b][2] // 2 + (b == len(BATCHES) - 1)


def dft_table():
    steps = np.arange(L, dtype=np.int64)
    window = (0.5 - 0.5 * np.cos(2.0 * np.pi * steps / L)).astype(np.float32)
    scale = np.sqrt(np.sum(window.astype(np.float64) ** 2)).astype(np.float32)
    theta = 2.0 * np.pi * ((BIN * steps) % L) / L
    cosine = np.round(np.cos(theta), 12)
    sine = np.round(np.sin(theta), 12)
    size = np.maximum(np.abs(cosine), np.abs(sine)).astype(np.float32)
    magnitude = (window * size / scale).astype(ml_dtypes.bfloat16).astype(np.float32)
    signs = [np.sign(cosine) if r < 4 else -np.sign(sine) for r in range(8)]
    return np.stack([magnitude] * 8), np.stack(signs)[:, :128].astype(np.float32)


def sine_cosine(turns):
    r = turns - jnp.round(turns)
    u = r * r
    s = SIN[-1]
    for coefficient in SIN[-2::-1]:
        s = s * u + coefficient
    s = s * r
    c = COS[-1]
    for coefficient in COS[-2::-1]:
        c = c * u + coefficient
    return s * c, 1.0 - s * s


def fitted():
    nodes = 0.125 - 0.125 * np.cos(np.pi * (np.arange(400) + 0.5) / 400)
    r = np.sqrt(nodes)
    sin_fit = np.polynomial.chebyshev.Chebyshev.fit(nodes, np.sqrt(2) * np.sin(np.pi * r) / r, 4, domain=[0, 0.25])
    cos_fit = np.polynomial.chebyshev.Chebyshev.fit(nodes, np.sqrt(2) * np.cos(np.pi * r), 4, domain=[0, 0.25])
    as_list = lambda fit: [float(v) for v in fit.convert(kind=np.polynomial.Polynomial).coef]
    return as_list(sin_fit), as_list(cos_fit)


SIN, COS = fitted()


def slot_of(grid):
    return (grid // 2 % NZ) * 4 + (grid // 16) * 2 + grid % 2


def grid_of(slot):
    return (slot // 2 % 2) * 16 + (slot // 4) * 2 + slot % 2


def kernel(
    samples, table_hbm, signs_hbm, mic_hbm, grid_hbm, out_ref,
    parts, table, signs, folded, mic, grid, mic_columns, own_spectra, gather, unpacked, weights, beams,
    load_sem, small_sem, gsend, grecv, bsend, brecv, there,
):
    me_mic = lax.axis_index("mic")
    me_grid = lax.axis_index("grid")
    me = slot_of(me_grid)
    height = 512 // PARTS

    smalls = [
        pltpu.make_async_copy(src, dst, small_sem.at[i])
        for i, (src, dst) in enumerate(
            [(table_hbm, table), (signs_hbm, signs), (mic_hbm, mic), (grid_hbm, grid)]
        )
    ]
    loads = [
        pltpu.make_async_copy(
            samples.at[0, pl.ds(p * height, height)],
            parts.at[pl.ds(p * height, height)],
            load_sem.at[p],
        )
        for p in range(PARTS)
    ]
    loads[0].start()
    smalls[0].start()
    for load in loads[1:]:
        load.start()
    for small in smalls[1:]:
        small.start()

    barrier = pltpu.get_barrier_semaphore()
    my_z = me // 4
    late = my_z // HALF
    own_base = late * CUBE

    def near(k):
        return own_base + lax.rem(me - own_base + k, CUBE)

    upwards = jnp.where(late == 1, 1, (me // 4) // 2)

    spot = lax.rem(me, 4)

    def across(k):
        z = jnp.where(upwards == 1, k // 4, HALF - 1 - k // 4)
        return CUBE - own_base + z * 4 + place(k % 4)

    def place(k):
        return (3 - spot, lax.rem(spot + 2, 4), spot + 1 - 2 * lax.rem(spot, 2), spot)[k]

    mic_steps = [(2, 1), (2, 0), (1, 1), (3, 1), (1, 0), (3, 0), (0, 1)]

    def mic_peer(k):
        step, other = mic_steps[k - 1]
        return lax.rem(me_mic // 2 + step, 4) * 2 + lax.rem(me_mic + other, 2)

    def signal(mic_index, slot):
        pl.semaphore_signal(
            barrier, inc=1, device_id=(mic_index, grid_of(slot)), device_id_type=MESH
        )

    @pl.when(late == 0)
    def _():
        for k in range(CUBE):
            signal(me_mic, across(k))

    for k in range(1, CUBE):
        signal(me_mic, near(k))
    for k in range(1, NMIC):
        signal(mic_peer(k), me)

    def spectra_copy(slot, semaphore):
        return pltpu.make_async_remote_copy(
            src_ref=own_spectra,
            dst_ref=gather.at[me],
            send_sem=gsend,
            recv_sem=grecv.at[semaphore],
            device_id=(me_mic, grid_of(slot)),
            device_id_type=MESH,
        )

    def spectra_wait(first, count, semaphore):
        return pltpu.make_async_remote_copy(
            src_ref=gather.at[pl.ds(first, count)],
            dst_ref=gather.at[pl.ds(first, count)],
            send_sem=gsend,
            recv_sem=grecv.at[semaphore],
            device_id=(me_mic, me_grid),
            device_id_type=MESH,
        )

    my_batch = me // 8

    fold = 64

    def fold_rows(i, carry):
        at = pl.multiple_of(i * fold, fold)
        total = jnp.zeros((fold, 128), jnp.float32)
        for t in range(0, L, 128):
            factor = jnp.concatenate([table[:, t : t + 128]] * (fold // 8), axis=0)
            total += parts[pl.ds(at, fold), t : t + 128].astype(jnp.float32) * factor
        folded[pl.ds(at, fold), :] = total
        return carry

    smalls[0].wait()
    for p in range(PARTS):
        loads[p].wait()
        lax.fori_loop(p * height // fold, (p + 1) * height // fold, fold_rows, 0)
    smalls[1].wait()
    total = lax.dot_general(
        signs[...],
        folded[...],
        (((1,), (1,)), ((), ())),
        preferred_element_type=jnp.float32,
        precision=lax.Precision.HIGHEST,
    )
    lane_block = lax.rem(lax.broadcasted_iota(jnp.int32, (8, 128), 0), 4)
    own = total[:, :128]
    for k in range(1, 4):
        own = jnp.where(lane_block == k, total[:, 128 * k : 128 * (k + 1)], own)
    own_spectra[...] = own.astype(jnp.bfloat16)
    pltpu.make_async_copy(own_spectra, gather.at[me], grecv.at[my_batch]).start()

    pl.semaphore_wait(barrier, CUBE - 1 + NMIC - 1 + late * CUBE)

    @pl.when(late == 1)
    def _():
        for k in range(CUBE):
            spectra_copy(across(k), my_batch).start()
        for z in range(HALF):
            @pl.when(me // 4 == (NZ - 1 if z < HALF // 2 else HALF))
            def _():
                pl.semaphore_signal(
                    there, inc=1, device_id=(me_mic, grid_of(z * 4 + spot)), device_id_type=MESH
                )

    for k in range(1, CUBE):
        spectra_copy(near(k), my_batch).start()

    smalls[2].wait()
    smalls[3].wait()
    mic_columns[...] = jnp.concatenate(
        [mic[...], jnp.zeros((5, 512), jnp.float32)], axis=0
    ).T
    gx = grid[0:1, :]
    gy = grid[1:2, :]
    gz = grid[2:3, :] + 1.5
    step = 32

    def steer(i, carry):
        at = pl.multiple_of(i * step, step)
        dx = gx - mic_columns[pl.ds(at, step), 0:1]
        dy = gy - mic_columns[pl.ds(at, step), 1:2]
        dz = gz - mic_columns[pl.ds(at, step), 2:3]
        dist = jnp.sqrt(dx * dx + dy * dy + dz * dz)
        sine, cosine = sine_cosine(dist * (WAVENUMBER / (2.0 * np.pi)))
        weights[pl.ds(at, step), :] = cosine.astype(jnp.bfloat16)
        weights[pl.ds(pl.multiple_of(at + 512, step), step), :] = sine.astype(jnp.bfloat16)
        return carry

    lax.fori_loop(0, 512 // step, steer, 0)

    def tile_of(beam, t):
        if beam.shape[0] == 8:
            return jnp.concatenate(
                [beam[:, 256 * t : 256 * t + 128], beam[:, 256 * t + 128 : 256 * (t + 1)]], axis=0
            )
        i, q = t // 4, t % 4
        return beam[16 * i : 16 * (i + 1), 128 * q : 128 * (q + 1)]

    def beam_copy(b, slot, peer):
        tiles = tiles_of(b)
        return pltpu.make_async_remote_copy(
            src_ref=beams.at[b, slot, pl.ds(0, tiles)],
            dst_ref=beams.at[b, slot, pl.ds(0, tiles)],
            send_sem=bsend.at[b],
            recv_sem=brecv.at[b],
            device_id=(peer, me_grid),
            device_id_type=MESH,
        )

    def beam_wait(b):
        return beam_copy(b, pl.ds(0, NMIC - 1), me_mic)

    last = len(BATCHES) - 1
    power = jnp.zeros((8, 128), jnp.float32)
    for b, (far, start, segs) in enumerate(BATCHES):
        if far:
            first = CUBE - own_base + jnp.where(upwards == 1, start, CUBE - start - segs)
        else:
            first = own_base + start
        if far and start == 0:
            @pl.when(late == 0)
            def _():
                pl.semaphore_wait(there, 1)
                for k in range(CUBE):
                    spectra_copy(across(k), my_batch).start()

        spectra_wait(first, segs, first // 8).wait_recv()
        tiles = tiles_of(b)
        block = gather[pl.ds(first, segs)].astype(jnp.float32)
        power += jnp.sum(block * block, axis=0)
        unpacked[:segs] = block
        real = jnp.concatenate([unpacked[:segs, k, :] for k in range(4)], axis=1)
        imag = jnp.concatenate([unpacked[:segs, 4 + k, :] for k in range(4)], axis=1)
        left = jnp.concatenate(
            [
                jnp.concatenate([real, -imag], axis=1),
                jnp.concatenate([imag, real], axis=1),
            ],
            axis=0,
        ).astype(jnp.bfloat16)
        beam = jnp.dot(left, weights[...], preferred_element_type=jnp.float32)
        for t in range(segs // 2):
            beams[b, me_mic, t] = tile_of(beam, t).astype(jnp.bfloat16)
        if b == len(BATCHES) - 1:
            high = power.astype(jnp.bfloat16)
            low = (power - high.astype(jnp.float32)).astype(jnp.bfloat16)
            beams[b, me_mic, tiles - 1] = jnp.concatenate([high, low], axis=0)
        for k in range(NMIC - 1):
            beam_copy(b, me_mic, jnp.where(me_mic <= k, k + 1, k)).start()

    spectra_wait(0, 2 * CUBE - 1, 0).wait_send()
    for b in range(last):
        beam_wait(b).wait_send()

    sums = [jnp.zeros((8, 128), jnp.float32) for _ in range(4)]
    for b, (far, start, segs) in enumerate(BATCHES):
        tiles = tiles_of(b)
        if b == last:
            beam_wait(b).wait_send()
        beam_wait(b).wait_recv()
        for t in range(segs // 2):
            whole = beams[b, 0, t].astype(jnp.float32)
            for j in range(1, NMIC):
                whole += beams[b, j, t].astype(jnp.float32)
            whole = whole * whole
            if segs == 4:
                sums[2 * t] += whole[:8]
                sums[2 * t + 1] += whole[8:]
            else:
                sums[t % 4] += whole[:8] + whole[8:]
    all_power = jnp.zeros((16, 128), jnp.float32)
    for j in range(NMIC):
        all_power += beams[last, j, tiles_of(last) - 1].astype(jnp.float32)
    all_power = jnp.sum(all_power)
    for q in range(4):
        line = (jnp.sum(sums[q], axis=0) - all_power) * (1.0 / (NGRID * 512 * NMIC))
        out_ref[pl.ds(128 * q, 128)] = line


def per_device(samples, mic_places, grid_places):
    hbm = pl.BlockSpec(memory_space=pltpu.HBM)
    table, signs = dft_table()
    return pl.pallas_call(
        kernel,
        out_shape=pltpu.VMEM((512,), jnp.float32),
        in_specs=[hbm] * 5,
        out_specs=pl.BlockSpec(memory_space=pltpu.VMEM),
        scratch_shapes=[
            pltpu.VMEM((512, L), jnp.bfloat16),
            pltpu.VMEM((8, L), jnp.float32),
            pltpu.VMEM((8, 128), jnp.float32),
            pltpu.VMEM((512, 128), jnp.float32),
            pltpu.VMEM((3, 512), jnp.float32),
            pltpu.VMEM((3, 512), jnp.float32),
            pltpu.VMEM((512, 8), jnp.float32),
            pltpu.VMEM((8, 128), jnp.bfloat16),
            pltpu.VMEM((NGRID, 8, 128), jnp.bfloat16),
            pltpu.VMEM((CUBE, 8, 128), jnp.float32),
            pltpu.VMEM((1024, 512), jnp.bfloat16),
            pltpu.VMEM((len(BATCHES), NMIC, 8, 16, 128), jnp.bfloat16),
            pltpu.SemaphoreType.DMA((PARTS,)),
            pltpu.SemaphoreType.DMA((4,)),
            pltpu.SemaphoreType.DMA,
            pltpu.SemaphoreType.DMA((4,)),
            pltpu.SemaphoreType.DMA((len(BATCHES),)),
            pltpu.SemaphoreType.DMA((len(BATCHES),)),
            pltpu.SemaphoreType.REGULAR,
        ],
        compiler_params=pltpu.CompilerParams(
            collective_id=0, has_side_effects=True, vmem_limit_bytes=60 * 1024 * 1024
        ),
    )(samples, jnp.asarray(table), jnp.asarray(signs), mic_places, grid_places)


def solution(mesh):
    in_specs = (P("grid", "mic", None), P(None, "mic"), P(None, "grid"))
    return jax.shard_map(
        per_device, mesh=mesh, in_specs=in_specs, out_specs=P("grid"), check_vma=False
    )
```

```python
import jax
import jax.numpy as jnp
import ml_dtypes
import numpy as np
from jax import lax
from jax.experimental import pallas as pl
from jax.experimental.pallas import tpu as pltpu
from jax.sharding import PartitionSpec as P

L = 4096
BIN = 512
WAVENUMBER = 120.0
MESH = pl.DeviceIdType.MESH

NMIC = 8
NGRID = 32
NZ = 8
PARTS = 4
HALF = 4
CUBE = 16
BATCHES = ((0, 0, 8), (0, 8, 8), (1, 0, 8), (1, 8, 8))


def tiles_of(b):
    return BATCHES[b][2] // 2 + (b == len(BATCHES) - 1)


def dft_table():
    steps = np.arange(L, dtype=np.int64)
    window = (0.5 - 0.5 * np.cos(2.0 * np.pi * steps / L)).astype(np.float32)
    scale = np.sqrt(np.sum(window.astype(np.float64) ** 2)).astype(np.float32)
    theta = 2.0 * np.pi * ((BIN * steps) % L) / L
    cosine = np.round(np.cos(theta), 12)
    sine = np.round(np.sin(theta), 12)
    size = np.maximum(np.abs(cosine), np.abs(sine)).astype(np.float32)
    magnitude = (window * size / scale).astype(ml_dtypes.bfloat16).astype(np.float32)
    signs = [np.sign(cosine) if r < 4 else -np.sign(sine) for r in range(8)]
    return np.stack([magnitude] * 8), np.stack(signs)[:, :128].astype(np.float32)


def sine_cosine(turns):
    r = turns - jnp.round(turns)
    u = r * r
    s = SIN[-1]
    for coefficient in SIN[-2::-1]:
        s = s * u + coefficient
    s = s * r
    c = COS[-1]
    for coefficient in COS[-2::-1]:
        c = c * u + coefficient
    return s * c, 1.0 - s * s


def fitted():
    nodes = 0.125 - 0.125 * np.cos(np.pi * (np.arange(400) + 0.5) / 400)
    r = np.sqrt(nodes)
    sin_fit = np.polynomial.chebyshev.Chebyshev.fit(nodes, np.sqrt(2) * np.sin(np.pi * r) / r, 4, domain=[0, 0.25])
    cos_fit = np.polynomial.chebyshev.Chebyshev.fit(nodes, np.sqrt(2) * np.cos(np.pi * r), 4, domain=[0, 0.25])
    as_list = lambda fit: [float(v) for v in fit.convert(kind=np.polynomial.Polynomial).coef]
    return as_list(sin_fit), as_list(cos_fit)


SIN, COS = fitted()


def slot_of(grid):
    return (grid // 2 % NZ) * 4 + (grid // 16) * 2 + grid % 2


def grid_of(slot):
    return (slot // 2 % 2) * 16 + (slot // 4) * 2 + slot % 2


def kernel(
    samples, table_hbm, signs_hbm, mic_hbm, grid_hbm, out_ref,
    parts, table, signs, folded, mic, grid, mic_columns, own_spectra, gather, unpacked, weights, beams,
    load_sem, small_sem, gsend, grecv, bsend, brecv, there,
):
    me_mic = lax.axis_index("mic")
    me_grid = lax.axis_index("grid")
    me = slot_of(me_grid)
    height = 512 // PARTS

    smalls = [
        pltpu.make_async_copy(src, dst, small_sem.at[i])
        for i, (src, dst) in enumerate(
            [(table_hbm, table), (signs_hbm, signs), (mic_hbm, mic), (grid_hbm, grid)]
        )
    ]
    loads = [
        pltpu.make_async_copy(
            samples.at[0, pl.ds(p * height, height)],
            parts.at[pl.ds(p * height, height)],
            load_sem.at[p],
        )
        for p in range(PARTS)
    ]
    loads[0].start()
    smalls[0].start()
    for load in loads[1:]:
        load.start()
    for small in smalls[1:]:
        small.start()

    barrier = pltpu.get_barrier_semaphore()
    my_z = me // 4
    late = my_z // HALF
    own_base = late * CUBE

    def near(k):
        return own_base + lax.rem(me - own_base + k, CUBE)

    upwards = jnp.where(late == 1, 1, (me // 4) // 2)

    spot = lax.rem(me, 4)

    def across(k):
        z = jnp.where(upwards == 1, k // 4, HALF - 1 - k // 4)
        return CUBE - own_base + z * 4 + place(k % 4)

    def place(k):
        return (3 - spot, lax.rem(spot + 2, 4), spot + 1 - 2 * lax.rem(spot, 2), spot)[k]

    mic_steps = [(2, 1), (2, 0), (1, 1), (3, 1), (1, 0), (3, 0), (0, 1)]

    def mic_peer(k):
        step, other = mic_steps[k - 1]
        return lax.rem(me_mic // 2 + step, 4) * 2 + lax.rem(me_mic + other, 2)

    def signal(mic_index, slot):
        pl.semaphore_signal(
            barrier, inc=1, device_id=(mic_index, grid_of(slot)), device_id_type=MESH
        )

    @pl.when(late == 0)
    def _():
        for k in range(CUBE):
            signal(me_mic, across(k))

    for k in range(1, CUBE):
        signal(me_mic, near(k))
    for k in range(1, NMIC):
        signal(mic_peer(k), me)

    def spectra_copy(slot, semaphore):
        return pltpu.make_async_remote_copy(
            src_ref=own_spectra,
            dst_ref=gather.at[me],
            send_sem=gsend,
            recv_sem=grecv.at[semaphore],
            device_id=(me_mic, grid_of(slot)),
            device_id_type=MESH,
        )

    def spectra_wait(first, count, semaphore):
        return pltpu.make_async_remote_copy(
            src_ref=gather.at[pl.ds(first, count)],
            dst_ref=gather.at[pl.ds(first, count)],
            send_sem=gsend,
            recv_sem=grecv.at[semaphore],
            device_id=(me_mic, me_grid),
            device_id_type=MESH,
        )

    my_batch = me // 8

    fold = 128

    def fold_rows(i, carry):
        at = pl.multiple_of(i * fold, fold)
        total = jnp.zeros((fold, 128), jnp.float32)
        for t in range(0, L, 128):
            factor = jnp.concatenate([table[:, t : t + 128]] * (fold // 8), axis=0)
            total += parts[pl.ds(at, fold), t : t + 128].astype(jnp.float32) * factor
        folded[pl.ds(at, fold), :] = total
        return carry

    smalls[0].wait()
    for p in range(PARTS):
        loads[p].wait()
        lax.fori_loop(p * height // fold, (p + 1) * height // fold, fold_rows, 0)
    smalls[1].wait()
    total = lax.dot_general(
        signs[...],
        folded[...],
        (((1,), (1,)), ((), ())),
        preferred_element_type=jnp.float32,
        precision=lax.Precision.HIGHEST,
    )
    lane_block = lax.rem(lax.broadcasted_iota(jnp.int32, (8, 128), 0), 4)
    own = total[:, :128]
    for k in range(1, 4):
        own = jnp.where(lane_block == k, total[:, 128 * k : 128 * (k + 1)], own)
    own_spectra[...] = own.astype(jnp.bfloat16)
    pltpu.make_async_copy(own_spectra, gather.at[me], grecv.at[my_batch]).start()

    pl.semaphore_wait(barrier, CUBE - 1 + NMIC - 1 + late * CUBE)

    @pl.when(late == 1)
    def _():
        for k in range(CUBE):
            spectra_copy(across(k), my_batch).start()
        for z in range(HALF):
            @pl.when(me // 4 == (NZ - 1 if z < HALF // 2 else HALF))
            def _():
                pl.semaphore_signal(
                    there, inc=1, device_id=(me_mic, grid_of(z * 4 + spot)), device_id_type=MESH
                )

    for k in range(1, CUBE):
        spectra_copy(near(k), my_batch).start()

    smalls[2].wait()
    smalls[3].wait()
    mic_columns[...] = jnp.concatenate(
        [mic[...], jnp.zeros((5, 512), jnp.float32)], axis=0
    ).T
    gx = grid[0:1, :]
    gy = grid[1:2, :]
    gz = grid[2:3, :] + 1.5
    step = 32

    def steer(i, carry):
        at = pl.multiple_of(i * step, step)
        dx = gx - mic_columns[pl.ds(at, step), 0:1]
        dy = gy - mic_columns[pl.ds(at, step), 1:2]
        dz = gz - mic_columns[pl.ds(at, step), 2:3]
        dist = jnp.sqrt(dx * dx + dy * dy + dz * dz)
        sine, cosine = sine_cosine(dist * (WAVENUMBER / (2.0 * np.pi)))
        weights[pl.ds(at, step), :] = cosine.astype(jnp.bfloat16)
        weights[pl.ds(pl.multiple_of(at + 512, step), step), :] = sine.astype(jnp.bfloat16)
        return carry

    lax.fori_loop(0, 512 // step, steer, 0)

    def tile_of(beam, t):
        if beam.shape[0] == 8:
            return jnp.concatenate(
                [beam[:, 256 * t : 256 * t + 128], beam[:, 256 * t + 128 : 256 * (t + 1)]], axis=0
            )
        i, q = t // 4, t % 4
        return beam[16 * i : 16 * (i + 1), 128 * q : 128 * (q + 1)]

    def beam_copy(b, slot, peer):
        tiles = tiles_of(b)
        return pltpu.make_async_remote_copy(
            src_ref=beams.at[b, slot, pl.ds(0, tiles)],
            dst_ref=beams.at[b, slot, pl.ds(0, tiles)],
            send_sem=bsend.at[b],
            recv_sem=brecv.at[b],
            device_id=(peer, me_grid),
            device_id_type=MESH,
        )

    def beam_wait(b):
        return beam_copy(b, pl.ds(0, NMIC - 1), me_mic)

    last = len(BATCHES) - 1
    power = jnp.zeros((8, 128), jnp.float32)
    for b, (far, start, segs) in enumerate(BATCHES):
        if far:
            first = CUBE - own_base + jnp.where(upwards == 1, start, CUBE - start - segs)
        else:
            first = own_base + start
        if far and start == 0:
            @pl.when(late == 0)
            def _():
                pl.semaphore_wait(there, 1)
                for k in range(CUBE):
                    spectra_copy(across(k), my_batch).start()

        spectra_wait(first, segs, first // 8).wait_recv()
        tiles = tiles_of(b)
        block = gather[pl.ds(first, segs)].astype(jnp.float32)
        power += jnp.sum(block * block, axis=0)
        unpacked[:segs] = block
        real = jnp.concatenate([unpacked[:segs, k, :] for k in range(4)], axis=1)
        imag = jnp.concatenate([unpacked[:segs, 4 + k, :] for k in range(4)], axis=1)
        left = jnp.concatenate(
            [
                jnp.concatenate([real, -imag], axis=1),
                jnp.concatenate([imag, real], axis=1),
            ],
            axis=0,
        ).astype(jnp.bfloat16)
        beam = jnp.dot(left, weights[...], preferred_element_type=jnp.float32)
        for t in range(segs // 2):
            beams[b, me_mic, t] = tile_of(beam, t).astype(jnp.bfloat16)
        if b == len(BATCHES) - 1:
            whole = jnp.full((8, 128), jnp.sum(power))
            high = whole.astype(jnp.bfloat16)
            low = (whole - high.astype(jnp.float32)).astype(jnp.bfloat16)
            beams[b, me_mic, tiles - 1] = jnp.concatenate([high, low], axis=0)
        def send(k, carry, b=b):
            beam_copy(b, me_mic, jnp.where(me_mic <= k, k + 1, k)).start()
            return carry

        lax.fori_loop(0, NMIC - 1, send, 0)

    spectra_wait(0, 2 * CUBE - 1, 0).wait_send()
    for b in range(last):
        beam_wait(b).wait_send()

    sums = [jnp.zeros((8, 128), jnp.float32) for _ in range(4)]
    for b, (far, start, segs) in enumerate(BATCHES):
        tiles = tiles_of(b)
        if b == last:
            beam_wait(b).wait_send()
        beam_wait(b).wait_recv()
        for t in range(segs // 2):
            whole = beams[b, 0, t].astype(jnp.float32)
            for j in range(1, NMIC):
                whole += beams[b, j, t].astype(jnp.float32)
            whole = whole * whole
            if segs == 4:
                sums[2 * t] += whole[:8]
                sums[2 * t + 1] += whole[8:]
            else:
                sums[t % 4] += whole[:8] + whole[8:]
    all_power = jnp.zeros((16, 128), jnp.float32)
    for j in range(NMIC):
        all_power += beams[last, j, tiles_of(last) - 1].astype(jnp.float32)
    all_power = all_power[0] + all_power[8]
    for q in range(4):
        line = (jnp.sum(sums[q], axis=0) - all_power) * (1.0 / (NGRID * 512 * NMIC))
        out_ref[pl.ds(128 * q, 128)] = line


def per_device(samples, mic_places, grid_places):
    hbm = pl.BlockSpec(memory_space=pltpu.HBM)
    table, signs = dft_table()
    return pl.pallas_call(
        kernel,
        out_shape=pltpu.VMEM((512,), jnp.float32),
        in_specs=[hbm] * 5,
        out_specs=pl.BlockSpec(memory_space=pltpu.VMEM),
        scratch_shapes=[
            pltpu.VMEM((512, L), jnp.bfloat16),
            pltpu.VMEM((8, L), jnp.float32),
            pltpu.VMEM((8, 128), jnp.float32),
            pltpu.VMEM((512, 128), jnp.float32),
            pltpu.VMEM((3, 512), jnp.float32),
            pltpu.VMEM((3, 512), jnp.float32),
            pltpu.VMEM((512, 8), jnp.float32),
            pltpu.VMEM((8, 128), jnp.bfloat16),
            pltpu.VMEM((NGRID, 8, 128), jnp.bfloat16),
            pltpu.VMEM((CUBE, 8, 128), jnp.float32),
            pltpu.VMEM((1024, 512), jnp.bfloat16),
            pltpu.VMEM((len(BATCHES), NMIC, 8, 16, 128), jnp.bfloat16),
            pltpu.SemaphoreType.DMA((PARTS,)),
            pltpu.SemaphoreType.DMA((4,)),
            pltpu.SemaphoreType.DMA,
            pltpu.SemaphoreType.DMA((4,)),
            pltpu.SemaphoreType.DMA((len(BATCHES),)),
            pltpu.SemaphoreType.DMA((len(BATCHES),)),
            pltpu.SemaphoreType.REGULAR,
        ],
        compiler_params=pltpu.CompilerParams(
            collective_id=0, has_side_effects=True, vmem_limit_bytes=60 * 1024 * 1024
        ),
    )(samples, jnp.asarray(table), jnp.asarray(signs), mic_places, grid_places)


def solution(mesh):
    in_specs = (P("grid", "mic", None), P(None, "mic"), P(None, "grid"))
    return jax.shard_map(
        per_device, mesh=mesh, in_specs=in_specs, out_specs=P("grid"), check_vma=False
    )
```

```python
import jax
import jax.numpy as jnp
import ml_dtypes
import numpy as np
from jax import lax
from jax.experimental import pallas as pl
from jax.experimental.pallas import tpu as pltpu
from jax.sharding import PartitionSpec as P

L = 4096
BIN = 512
WAVENUMBER = 120.0
MESH = pl.DeviceIdType.MESH

NMIC = 8
NGRID = 32
NZ = 8
PARTS = 4
HALF = 4
CUBE = 16
BATCHES = ((0, 0, 8), (0, 8, 8), (1, 0, 8), (1, 8, 8))


def tiles_of(b):
    return BATCHES[b][2] // 2 + (b == len(BATCHES) - 1)


def dft_table():
    steps = np.arange(L, dtype=np.int64)
    window = (0.5 - 0.5 * np.cos(2.0 * np.pi * steps / L)).astype(np.float32)
    scale = np.sqrt(np.sum(window.astype(np.float64) ** 2)).astype(np.float32)
    theta = 2.0 * np.pi * ((BIN * steps) % L) / L
    cosine = np.round(np.cos(theta), 12)
    sine = np.round(np.sin(theta), 12)
    size = np.maximum(np.abs(cosine), np.abs(sine)).astype(np.float32)
    magnitude = (window * size / scale).astype(ml_dtypes.bfloat16).astype(np.float32)
    signs = [np.sign(cosine) if r < 4 else -np.sign(sine) for r in range(8)]
    return np.stack([magnitude] * 8), np.stack(signs)[:, :128].astype(np.float32)


def sine_cosine(turns):
    r = turns - jnp.round(turns)
    u = r * r
    s = SIN[-1]
    for coefficient in SIN[-2::-1]:
        s = s * u + coefficient
    s = s * r
    c = COS[-1]
    for coefficient in COS[-2::-1]:
        c = c * u + coefficient
    return s * c, 1.0 - s * s


def fitted():
    nodes = 0.125 - 0.125 * np.cos(np.pi * (np.arange(400) + 0.5) / 400)
    r = np.sqrt(nodes)
    sin_fit = np.polynomial.chebyshev.Chebyshev.fit(nodes, np.sqrt(2) * np.sin(np.pi * r) / r, 4, domain=[0, 0.25])
    cos_fit = np.polynomial.chebyshev.Chebyshev.fit(nodes, np.sqrt(2) * np.cos(np.pi * r), 4, domain=[0, 0.25])
    as_list = lambda fit: [float(v) for v in fit.convert(kind=np.polynomial.Polynomial).coef]
    return as_list(sin_fit), as_list(cos_fit)


SIN, COS = fitted()


def slot_of(grid):
    return (grid // 2 % NZ) * 4 + (grid // 16) * 2 + grid % 2


def grid_of(slot):
    return (slot // 2 % 2) * 16 + (slot // 4) * 2 + slot % 2


def kernel(
    samples, table_hbm, signs_hbm, mic_hbm, grid_hbm, out_ref,
    parts, table, signs, folded, mic, grid, mic_columns, own_spectra, gather, unpacked, weights, beams,
    load_sem, small_sem, gsend, grecv, bsend, brecv, there,
):
    me_mic = lax.axis_index("mic")
    me_grid = lax.axis_index("grid")
    me = slot_of(me_grid)
    height = 512 // PARTS

    smalls = [
        pltpu.make_async_copy(src, dst, small_sem.at[i])
        for i, (src, dst) in enumerate(
            [(table_hbm, table), (signs_hbm, signs), (mic_hbm, mic), (grid_hbm, grid)]
        )
    ]
    loads = [
        pltpu.make_async_copy(
            samples.at[0, pl.ds(p * height, height)],
            parts.at[pl.ds(p * height, height)],
            load_sem.at[p],
        )
        for p in range(PARTS)
    ]
    loads[0].start()
    smalls[0].start()
    for load in loads[1:]:
        load.start()
    for small in smalls[1:]:
        small.start()

    barrier = pltpu.get_barrier_semaphore()
    my_z = me // 4
    late = my_z // HALF
    own_base = late * CUBE

    def near(k):
        return own_base + lax.rem(me - own_base + k, CUBE)

    upwards = jnp.where(late == 1, 1, (me // 4) // 2)

    spot = lax.rem(me, 4)

    def across(k):
        z = jnp.where(upwards == 1, k // 4, HALF - 1 - k // 4)
        return CUBE - own_base + z * 4 + place(k % 4)

    def place(k):
        return (3 - spot, lax.rem(spot + 2, 4), spot + 1 - 2 * lax.rem(spot, 2), spot)[k]

    mic_steps = [(2, 1), (2, 0), (1, 1), (3, 1), (1, 0), (3, 0), (0, 1)]

    def mic_peer(k):
        step, other = mic_steps[k - 1]
        return lax.rem(me_mic // 2 + step, 4) * 2 + lax.rem(me_mic + other, 2)

    def signal(mic_index, slot):
        pl.semaphore_signal(
            barrier, inc=1, device_id=(mic_index, grid_of(slot)), device_id_type=MESH
        )

    @pl.when(late == 0)
    def _():
        for k in range(CUBE):
            signal(me_mic, across(k))

    for k in range(1, CUBE):
        signal(me_mic, near(k))
    for k in range(1, NMIC):
        signal(mic_peer(k), me)

    def spectra_copy(slot, semaphore):
        return pltpu.make_async_remote_copy(
            src_ref=own_spectra,
            dst_ref=gather.at[me],
            send_sem=gsend,
            recv_sem=grecv.at[semaphore],
            device_id=(me_mic, grid_of(slot)),
            device_id_type=MESH,
        )

    def spectra_wait(first, count, semaphore):
        return pltpu.make_async_remote_copy(
            src_ref=gather.at[pl.ds(first, count)],
            dst_ref=gather.at[pl.ds(first, count)],
            send_sem=gsend,
            recv_sem=grecv.at[semaphore],
            device_id=(me_mic, me_grid),
            device_id_type=MESH,
        )

    my_batch = me // 8

    fold = 128

    def fold_rows(i, carry):
        at = pl.multiple_of(i * fold, fold)
        total = jnp.zeros((fold, 128), jnp.float32)
        for t in range(0, L, 128):
            factor = jnp.concatenate([table[:, t : t + 128]] * (fold // 8), axis=0)
            total += parts[pl.ds(at, fold), t : t + 128].astype(jnp.float32) * factor
        folded[pl.ds(at, fold), :] = total
        return carry

    smalls[0].wait()
    for p in range(PARTS):
        loads[p].wait()
        lax.fori_loop(p * height // fold, (p + 1) * height // fold, fold_rows, 0)
    smalls[1].wait()
    total = lax.dot_general(
        signs[...],
        folded[...],
        (((1,), (1,)), ((), ())),
        preferred_element_type=jnp.float32,
        precision=lax.Precision.HIGHEST,
    )
    lane_block = lax.rem(lax.broadcasted_iota(jnp.int32, (8, 128), 0), 4)
    own = total[:, :128]
    for k in range(1, 4):
        own = jnp.where(lane_block == k, total[:, 128 * k : 128 * (k + 1)], own)
    own_spectra[...] = own.astype(jnp.bfloat16)
    pltpu.make_async_copy(own_spectra, gather.at[me], grecv.at[my_batch]).start()

    pl.semaphore_wait(barrier, CUBE - 1 + NMIC - 1 + late * CUBE)

    @pl.when(late == 1)
    def _():
        for k in range(CUBE):
            spectra_copy(across(k), my_batch).start()
        for z in range(HALF):
            @pl.when(me // 4 == (NZ - 1 if z < HALF // 2 else HALF))
            def _():
                pl.semaphore_signal(
                    there, inc=1, device_id=(me_mic, grid_of(z * 4 + spot)), device_id_type=MESH
                )

    for k in range(1, CUBE):
        spectra_copy(near(k), my_batch).start()

    smalls[2].wait()
    smalls[3].wait()
    mic_columns[...] = jnp.concatenate(
        [mic[...], jnp.zeros((5, 512), jnp.float32)], axis=0
    ).T
    gx = grid[0:1, :]
    gy = grid[1:2, :]
    gz = grid[2:3, :] + 1.5
    step = 32

    def steer(i, carry):
        at = pl.multiple_of(i * step, step)
        dx = gx - mic_columns[pl.ds(at, step), 0:1]
        dy = gy - mic_columns[pl.ds(at, step), 1:2]
        dz = gz - mic_columns[pl.ds(at, step), 2:3]
        dist = jnp.sqrt(dx * dx + dy * dy + dz * dz)
        sine, cosine = sine_cosine(dist * (WAVENUMBER / (2.0 * np.pi)))
        weights[pl.ds(at, step), :] = cosine.astype(jnp.bfloat16)
        weights[pl.ds(pl.multiple_of(at + 512, step), step), :] = sine.astype(jnp.bfloat16)
        return carry

    lax.fori_loop(0, 512 // step, steer, 0)

    def tile_of(beam, t):
        if beam.shape[0] == 8:
            return jnp.concatenate(
                [beam[:, 256 * t : 256 * t + 128], beam[:, 256 * t + 128 : 256 * (t + 1)]], axis=0
            )
        i, q = t // 4, t % 4
        return beam[16 * i : 16 * (i + 1), 128 * q : 128 * (q + 1)]

    def beam_copy(b, slot, peer):
        tiles = tiles_of(b)
        return pltpu.make_async_remote_copy(
            src_ref=beams.at[b, slot, pl.ds(0, tiles)],
            dst_ref=beams.at[b, slot, pl.ds(0, tiles)],
            send_sem=bsend.at[b],
            recv_sem=brecv.at[b],
            device_id=(peer, me_grid),
            device_id_type=MESH,
        )

    def beam_wait(b):
        return beam_copy(b, pl.ds(0, NMIC - 1), me_mic)

    last = len(BATCHES) - 1
    power = jnp.zeros((8, 128), jnp.float32)
    for b, (far, start, segs) in enumerate(BATCHES):
        if far:
            first = CUBE - own_base + jnp.where(upwards == 1, start, CUBE - start - segs)
        else:
            first = own_base + start
        if far and start == 0:
            @pl.when(late == 0)
            def _():
                pl.semaphore_wait(there, 1)
                for k in range(CUBE):
                    spectra_copy(across(k), my_batch).start()

        spectra_wait(first, segs, first // 8).wait_recv()
        tiles = tiles_of(b)
        block = gather[pl.ds(first, segs)].astype(jnp.float32)
        power += jnp.sum(block * block, axis=0)
        unpacked[:segs] = block
        real = jnp.concatenate([unpacked[:segs, k, :] for k in range(4)], axis=1)
        imag = jnp.concatenate([unpacked[:segs, 4 + k, :] for k in range(4)], axis=1)
        left = jnp.concatenate(
            [
                jnp.concatenate([real, -imag], axis=1),
                jnp.concatenate([imag, real], axis=1),
            ],
            axis=0,
        ).astype(jnp.bfloat16)
        beam = jnp.dot(left, weights[...], preferred_element_type=jnp.float32)
        for t in range(segs // 2):
            beams[b, me_mic, t] = tile_of(beam, t).astype(jnp.bfloat16)
        if b == len(BATCHES) - 1:
            whole = jnp.full((8, 128), jnp.sum(power))
            high = whole.astype(jnp.bfloat16)
            low = (whole - high.astype(jnp.float32)).astype(jnp.bfloat16)
            beams[b, me_mic, tiles - 1] = jnp.concatenate([high, low], axis=0)
        def send(k, carry, b=b):
            at = lax.rem(me_mic, 2) * 4 + me_mic // 2
            u = jnp.where(at <= k, k + 1, k)
            beam_copy(b, me_mic, lax.rem(u, 4) * 2 + u // 4).start()
            return carry

        lax.fori_loop(0, NMIC - 1, send, 0)

    spectra_wait(0, 2 * CUBE - 1, 0).wait_send()
    for b in range(last):
        beam_wait(b).wait_send()

    sums = [jnp.zeros((8, 128), jnp.float32) for _ in range(4)]
    for b, (far, start, segs) in enumerate(BATCHES):
        tiles = tiles_of(b)
        if b == last:
            beam_wait(b).wait_send()
        beam_wait(b).wait_recv()
        for t in range(segs // 2):
            whole = beams[b, 0, t].astype(jnp.float32)
            for j in range(1, NMIC):
                whole += beams[b, j, t].astype(jnp.float32)
            whole = whole * whole
            if segs == 4:
                sums[2 * t] += whole[:8]
                sums[2 * t + 1] += whole[8:]
            else:
                sums[t % 4] += whole[:8] + whole[8:]
    all_power = jnp.zeros((16, 128), jnp.float32)
    for j in range(NMIC):
        all_power += beams[last, j, tiles_of(last) - 1].astype(jnp.float32)
    all_power = all_power[0] + all_power[8]
    for q in range(4):
        line = jnp.sum(sums[q], axis=0) - all_power
        out_ref[pl.ds(128 * q, 128)] = line


def per_device(samples, mic_places, grid_places):
    hbm = pl.BlockSpec(memory_space=pltpu.HBM)
    table, signs = dft_table()
    beam_map = pl.pallas_call(
        kernel,
        out_shape=pltpu.VMEM((512,), jnp.float32),
        in_specs=[hbm] * 5,
        out_specs=pl.BlockSpec(memory_space=pltpu.VMEM),
        scratch_shapes=[
            pltpu.VMEM((512, L), jnp.bfloat16),
            pltpu.VMEM((8, L), jnp.float32),
            pltpu.VMEM((8, 128), jnp.float32),
            pltpu.VMEM((512, 128), jnp.float32),
            pltpu.VMEM((3, 512), jnp.float32),
            pltpu.VMEM((3, 512), jnp.float32),
            pltpu.VMEM((512, 8), jnp.float32),
            pltpu.VMEM((8, 128), jnp.bfloat16),
            pltpu.VMEM((NGRID, 8, 128), jnp.bfloat16),
            pltpu.VMEM((CUBE, 8, 128), jnp.float32),
            pltpu.VMEM((1024, 512), jnp.bfloat16),
            pltpu.VMEM((len(BATCHES), NMIC, 8, 16, 128), jnp.bfloat16),
            pltpu.SemaphoreType.DMA((PARTS,)),
            pltpu.SemaphoreType.DMA((4,)),
            pltpu.SemaphoreType.DMA,
            pltpu.SemaphoreType.DMA((4,)),
            pltpu.SemaphoreType.DMA((len(BATCHES),)),
            pltpu.SemaphoreType.DMA((len(BATCHES),)),
            pltpu.SemaphoreType.REGULAR,
        ],
        compiler_params=pltpu.CompilerParams(
            collective_id=0, has_side_effects=True, vmem_limit_bytes=60 * 1024 * 1024
        ),
    )(samples, jnp.asarray(table), jnp.asarray(signs), mic_places, grid_places)
    return beam_map * (1.0 / (NGRID * 512 * NMIC))


def solution(mesh):
    in_specs = (P("grid", "mic", None), P(None, "mic"), P(None, "grid"))
    return jax.shard_map(
        per_device, mesh=mesh, in_specs=in_specs, out_specs=P("grid"), check_vma=False
    )
```
